128 devices in a mesh: dp: 2 (over z_lo), ctx: 32 (over x, y, core), tensor: 2 (over z_hi).
Axes of the slice: x: 4, y: 4, z: 4 (z_hi: 2, z_lo: 2; z = z_hi * 2 + z_lo), core: 2. Of those that a mesh axis runs over, the one named last changes fastest.
Arguments:
- layer_input: bfloat16 [2, 4352, 384], P('dp', 'ctx'), may hold values from -6 to 6
- valid_count: int32 [2], P('dp'), may hold values from 4217 to 4352, as said below
- cotangent: bfloat16 [2, 4352, 384], P('dp', 'ctx'), may hold values from -6 to 6
- ln1_gain: bfloat16 [384], P('dp'), may hold values from 0.099609375 to 1.8984375
- ln1_bias: bfloat16 [384], P('dp'), may hold values from -3 to 3
- w_query: bfloat16 [384, 384], P('dp', 'tensor'), may hold values from -0.4375 to 0.4375
- b_query: bfloat16 [384], P(('tensor', 'dp')), may hold values from -3 to 3
- w_key: bfloat16 [384, 384], P('dp', 'tensor'), may hold values from -0.4375 to 0.4375
- w_value: bfloat16 [384, 384], P('dp', 'tensor'), may hold values from -0.3125 to 0.3125
- b_value: bfloat16 [384], P(('tensor', 'dp')), may hold values from -3 to 3
- w_out: bfloat16 [384, 384], P('tensor', 'dp'), may hold values from -2.5 to 2.5
- b_out: bfloat16 [384], P('dp'), may hold values from -3 to 3
- ln2_gain: bfloat16 [384], P('dp'), may hold values from 0.099609375 to 1.8984375
- ln2_bias: bfloat16 [384], P('dp'), may hold values from -3 to 3
- w_up: bfloat16 [384, 1536], P('dp', 'tensor'), may hold values from -0.3125 to 0.3125
- b_up: bfloat16 [1536], P(('tensor', 'dp')), may hold values from -3 to 3
- w_down: bfloat16 [1536, 384], P('tensor', 'dp'), may hold values from -0.15625 to 0.15625
- b_down: bfloat16 [384], P('dp'), may hold values from -3 to 3
Outputs:
- layer_output: bfloat16 [2, 4352, 384], P('dp', 'ctx')
- grad_input: float32 [2, 4352, 384], P('dp', 'ctx')
- grad_ln1_gain: float32 [384], P('dp')
- grad_ln1_bias: float32 [384], P('dp')
- grad_w_query: float32 [384, 384], P('dp', 'tensor')
- grad_b_query: float32 [384], P(('tensor', 'dp'))
- grad_w_key: float32 [384, 384], P('dp', 'tensor')
- grad_w_value: float32 [384, 384], P('dp', 'tensor')
- grad_b_value: float32 [384], P(('tensor', 'dp'))
- grad_w_out: float32 [384, 384], P('tensor', 'dp')
- grad_b_out: float32 [384], P('dp')
- grad_ln2_gain: float32 [384], P('dp')
- grad_ln2_bias: float32 [384], P('dp')
- grad_w_up: float32 [384, 1536], P('dp', 'tensor')
- grad_b_up: float32 [1536], P(('tensor', 'dp'))
- grad_w_down: float32 [1536, 384], P('tensor', 'dp')
- grad_b_down: float32 [384], P('dp')
The draws below stay inside these ranges and needn't reach their ends.
Inputs may be any that keep to these rules, and one draw needn't show every extreme that they name: `valid_count`: every image has a valid token in the last 136 positions.
All inputs are finite; a program needn't handle non-finite values.
Results may differ from the reference program's by a relative error of at most 0.03.
Values may be sent and summed in bfloat16 or wider, within the bound.
A program may use at most 64 MiB of HBM per device.

```python
import jax
import jax.numpy as jnp
from jax import lax

D = 384
HEADS = 6
HEAD = 64
FF = 1536
TOK_DEV = 136
SEQ = 4352
IMAGES = 2


def draw_valid_count(key, part):
    key = jax.random.fold_in(key, 11)
    first, second = jax.random.split(key)
    short = jax.random.randint(first, (IMAGES,), 0, TOK_DEV)
    chosen = jax.random.randint(second, (), 0, IMAGES)
    missing = jnp.where(jnp.arange(IMAGES) == chosen, 0, short)
    return (SEQ - missing).astype(jnp.int32)


def steps_of(key, dims, pieces, smallest, largest):
    level, own = 1.0, jax.random.fold_in(key, 6)
    for axis_at, shards_of in pieces:
        steps = jnp.exp(jax.random.uniform(jax.random.fold_in(own, axis_at), (shards_of,), jnp.float32, smallest / len(pieces), largest / len(pieces)))
        level = level * jnp.repeat(steps, dims[axis_at] // shards_of).reshape([-1 if axis == axis_at else 1 for axis in range(len(dims))])
    return level


def gaussian(key, extent, scale, most, cuts=(), held_as=jnp.bfloat16):
    gain = steps_of(key, extent, cuts, -0.22, 0.18) if cuts else 1.0
    entries = jax.random.normal(key, extent, jnp.float32) * scale * gain
    return jnp.minimum(jnp.maximum(entries, -most), most).astype(held_as)


def setup_inputs(seed: int = 0) -> dict:
    arg_keys = jax.random.split(jax.random.key(seed), 19)
    return {
        "layer_input": gaussian(arg_keys[0], (IMAGES, SEQ, D), 1.0, 6.0, ((0, 2), (1, 32))),
        "valid_count": draw_valid_count(jax.random.fold_in(arg_keys[18], 71), 0),
        "cotangent": gaussian(arg_keys[2], (IMAGES, SEQ, D), 1.0, 6.0, ((0, 2), (1, 32))),
        "ln1_gain": jnp.clip(1.0 + 0.18 * jax.random.normal(arg_keys[3], (D,), jnp.float32), 0.099609375, 1.8984375).astype(jnp.bfloat16),
        "ln1_bias": gaussian(arg_keys[4], (D,), 0.5, 3.0, ((0, 2),)),
        "w_query": gaussian(arg_keys[5], (D, D), (D // 2) ** -0.5, 0.4375, ((0, 2), (1, 2))),
        "b_query": gaussian(arg_keys[6], (D,), 0.5, 3.0, ((0, 4),)),
        "w_key": gaussian(arg_keys[7], (D, D), (D // 2) ** -0.5, 0.4375, ((0, 2), (1, 2))),
        "w_value": gaussian(arg_keys[8], (D, D), D ** -0.5, 0.3125, ((0, 2), (1, 2))),
        "b_value": gaussian(arg_keys[9], (D,), 0.5, 3.0, ((0, 4),)),
        "w_out": gaussian(arg_keys[10], (D, D), (max(1, D // 64)) ** -0.5, 2.5, ((0, 2), (1, 2))),
        "b_out": gaussian(arg_keys[11], (D,), 0.5, 3.0, ((0, 2),)),
        "ln2_gain": jnp.clip(1.0 + 0.18 * jax.random.normal(arg_keys[12], (D,), jnp.float32), 0.099609375, 1.8984375).astype(jnp.bfloat16),
        "ln2_bias": gaussian(arg_keys[13], (D,), 0.5, 3.0, ((0, 2),)),
        "w_up": gaussian(arg_keys[14], (D, FF), D ** -0.5, 0.3125, ((0, 2), (1, 2))),
        "b_up": gaussian(arg_keys[15], (FF,), 0.5, 3.0, ((0, 4),)),
        "w_down": gaussian(arg_keys[16], (FF, D), FF ** -0.5, 0.15625, ((0, 2), (1, 2))),
        "b_down": gaussian(arg_keys[17], (D,), 0.5, 3.0, ((0, 2),)),
    }


@jax.custom_vjp
def low(v):
    return lax.optimization_barrier(v.astype(jnp.bfloat16)).astype(jnp.float32)

@jax.custom_vjp
def low_back(v):
    return v

def low_keep(v):
    return (low(v), None)

def low_pass(kept, grad):
    return (grad,)

def back_keep(v):
    return (v, None)

def back_low(kept, grad):
    return (low(grad),)
low.defvjp(low_keep, low_pass)
low_back.defvjp(back_keep, back_low)
EPSILON = 1e-06
HIGH = lax.Precision.HIGHEST

def normalize(rows):
    center = rows - lax.optimization_barrier(jnp.mean(rows, axis=-1, keepdims=True))
    spread = lax.optimization_barrier(jnp.mean(center * center, axis=-1, keepdims=True))
    return center * lax.rsqrt(spread + EPSILON)

def matmul_high(left, right):
    return jnp.dot(left, right, precision=HIGH, preferred_element_type=jnp.float32)

def image_layer(tokens, limit, params):
    gain1, shift1, wquery, bquery, wkey, wvalue, bvalue, wout, bout, gain2, shift2, wup, bup, wdown, bdown = params
    normed1 = low(normalize(tokens) * gain1 + shift1)
    queries = low(low_back(matmul_high(normed1, wquery) + bquery))
    keys = low(low_back(matmul_high(normed1, wkey)))
    values = low(low_back(matmul_high(normed1, wvalue) + bvalue))
    keys_ok = jnp.arange(SEQ) < limit
    key_heads = keys.reshape(SEQ, HEADS, HEAD)
    value_heads = values.reshape(SEQ, HEADS, HEAD)

    def attend(query_block):
        scores = jnp.einsum('qhe,khe->hqk', query_block, key_heads, precision=HIGH) * HEAD ** (-0.5)
        scores = low_back(scores)
        scores = jnp.where(keys_ok[None, None, :], scores, -1e+30)
        probs = low(jax.nn.softmax(scores, axis=-1))
        mixed = jnp.einsum('hqk,khe->qhe', probs, value_heads, precision=HIGH)
        return mixed.reshape(query_block.shape[0], D)
    blocks = queries.reshape(SEQ // TOK_DEV, TOK_DEV, HEADS, HEAD)
    attended = lax.map(jax.checkpoint(attend), blocks).reshape(SEQ, D)
    attended = low(low_back(attended))
    hidden1 = tokens + low_back(matmul_high(attended, wout)) + bout
    normed2 = low(normalize(hidden1) * gain2 + shift2)
    upper = low_back(matmul_high(normed2, wup) + bup)
    active = low(jax.nn.gelu(upper, approximate=False))
    return hidden1 + matmul_high(active, wdown) + bdown

def reference(layer_input, valid_count, cotangent, ln1_gain, ln1_bias, w_query, b_query, w_key, w_value, b_value, w_out, b_out, ln2_gain, ln2_bias, w_up, b_up, w_down, b_down):
    params = tuple((item.astype(jnp.float32) for item in (ln1_gain, ln1_bias, w_query, b_query, w_key, w_value, b_value, w_out, b_out, ln2_gain, ln2_bias, w_up, b_up, w_down, b_down)))
    start_rows = layer_input.astype(jnp.float32)

    def forward(rows_in, weights):
        return jax.vmap(lambda image, limit: image_layer(image, limit, weights))(rows_in, valid_count)
    result, pullback = jax.vjp(forward, start_rows, params)
    rows_ok = (jnp.arange(SEQ)[None, :] < valid_count[:, None]).astype(jnp.float32)
    grad_rows, grads = pullback(cotangent.astype(jnp.float32) * rows_ok[:, :, None])
    return (result.astype(jnp.bfloat16), grad_rows, grads[0], grads[1], grads[2], grads[3], grads[4], grads[5], grads[6], grads[7], grads[8], grads[9], grads[10], grads[11], grads[12], grads[13], grads[14])
```

```python
import jax
import jax.numpy as jnp
from jax import lax
from jax.experimental import pallas as pl
from jax.experimental.pallas import tpu as pltpu
from jax.sharding import PartitionSpec as P

F32 = jnp.float32
BF16 = jnp.bfloat16
MESH = pl.DeviceIdType.MESH

HEAD = 64
OWN = 136
PAD = 144
WIDE = 384
HALF = 192
HID = 768
GROUP = 4 * PAD
STACK = 3 * PAD
EPSILON = 1e-06
UNITS_1 = 80
UNITS_2 = 32
UNITS_3 = 16
NORM_ROWS = 864
COPIES = 288
VMEM_BYTES = 63 * 1024 * 1024
SMALL = (HALF, HALF, HALF, HALF, HALF, HALF, 96, 96, WIDE)


def mm(left, right):
    return lax.dot_general(left, right, (((1,), (0,)), ((), ())), preferred_element_type=F32)


def mm_nt(left, right):
    return lax.dot_general(left, right, (((1,), (1,)), ((), ())), preferred_element_type=F32)


def mm_tn(left, right):
    return lax.dot_general(left, right, (((0,), (0,)), ((), ())), preferred_element_type=F32)


def rows(start, size):
    return pl.ds(pl.multiple_of(start, 16), size)


def lanes_of(shape):
    return lax.broadcasted_iota(jnp.int32, shape, 1)


def widen(value):
    return jnp.concatenate([value, jnp.zeros((value.shape[0], 64), value.dtype)], axis=1)


def three_parts(value):
    high = value.astype(BF16).astype(F32)
    rest = value - high
    middle = rest.astype(BF16).astype(F32)
    return high, middle, (rest - middle).astype(BF16).astype(F32)


def layer_kernel(
    x_ref, count_ref, cot_ref, g1_ref, s1_ref, wq_ref, bq_ref, wk_ref, wv_ref, bv_ref, wo_ref, bo_ref,
    g2_ref, s2_ref, wu_ref, bu_ref, wd_ref, bd_ref,
    y_ref, gx_ref, f1_ref, f2_ref, f3_ref,
    send_sems, recv_sems, load_sems,
    wqf, wkf, wvf, wof, wuf, wdt, woc, vec, vfull, xin, cotin, *rest_refs
):
    small_refs, rest_refs = rest_refs[: len(SMALL)], rest_refs[len(SMALL) :]
    (
    kvx, qx, nkv, nq, dob, picker, wall, wall_t, qall, qbig, kbuf, vbuf, kt, vt, bias, pt, mrow, om, omr, dobig, factor, gscore, acck, accv, dqm, dqr,
    gsib, gsibr, gown, gy, gyr,
    xh1, rstd1, n1, gout, attf, attx, hid, xh2, rstd2, n2, act, gup, gn2p, gn1x, ghid, gnq,
    src1, sib1, s01, ar1, s11, br1, fin1,
    src2, sib2, s02, all2, fin2, src3, sib3, s03, all3, fin3, tr2, yout, gxout,
    ) = rest_refs
    d, n, t = lax.axis_index("dp"), lax.axis_index("ctx"), lax.axis_index("tensor")
    c, chip = n % 2, n // 2
    chip_x, chip_y = chip // 4, chip % 4
    a, b = chip_x * (1 - c) + chip_y * c, chip_y * (1 - c) + chip_x * c

    def dev(to_a, to_b):
        to_x, to_y = to_a * (1 - c) + to_b * c, to_b * (1 - c) + to_a * c
        return (d, (to_x * 4 + to_y) * 2 + c, t)

    d_other, t_other = 1 - d, 1 - t
    sib = (d, n + 1 - 2 * c, t)
    z_dp, z_tensor, z_both = (d_other, n, t), (d, n, t_other), (d_other, n, t_other)
    a_up, a_down, a_far = (a + 1) % 4, (a + 3) % 4, (a + 2) % 4
    b_up, b_down, b_far = (b + 1) % 4, (b + 3) % 4, (b + 2) % 4

    def by_place(to_x, to_y):
        return (d, (to_x * 4 + to_y) * 2 + c, t)

    xs = [chip_x, (chip_x + 3) % 4, (chip_x + 1) % 4, (chip_x + 2) % 4]
    ys = [chip_y, (chip_y + 3) % 4, (chip_y + 1) % 4, (chip_y + 2) % 4]
    x_dev, y_dev = [by_place(x, chip_y) for x in xs], [by_place(chip_x, y) for y in ys]

    barrier = pltpu.get_barrier_semaphore()
    a_plus, a_minus, b_plus, b_minus = dev(a_up, b), dev(a_down, b), dev(a, b_up), dev(a, b_down)
    a_across, b_across = dev(a_far, b), dev(a, b_far)
    along_a = ((a_up, a_plus), (a_far, a_across), (a_down, a_minus))
    along_b = ((b_up, b_plus), (b_far, b_across), (b_down, b_minus))
    other_plane = [(d_other, device[1], t) for device in (z_dp, b_plus, b_across, b_minus)]
    tensor_sib = (d, sib[1], t_other)
    everywhere = [
        (plane, place, (d, d_other)[plane], dev(place[0], place[1]))
        for plane in range(2)
        for place in [(to_a, to_b) for to_a in (a, a_up, a_far, a_down) for to_b in (b, b_up, b_far, b_down)]
    ][1:]
    everywhere = [(i + 1, plane, place, (to_d, device[1], t)) for i, (plane, place, to_d, device) in enumerate(everywhere)]
    partners = [sib, z_tensor, z_both, tensor_sib] + [device for _, _, _, device in everywhere]
    for partner in partners:
        pl.semaphore_signal(barrier, inc=1, device_id=partner, device_id_type=MESH)

    sent = []

    class Copy:
        def __init__(self, source, target, device, k=None):
            self.parts = source, target, device
            self.k = k
            if k is None:
                self.k = len(sent)
                sent.append(self)
            self.made().start()

        def made(self):
            source, target, device = (part() if callable(part) else part for part in self.parts)
            return pltpu.make_async_remote_copy(
                src_ref=source, dst_ref=target, send_sem=send_sems.at[self.k], recv_sem=recv_sems.at[self.k],
                device_id=device, device_id_type=MESH,
            )

        def wait_recv(self):
            self.made().wait_recv()

        def wait_send(self):
            self.made().wait_send()

    def send(source, target, device):
        return Copy(source, target, device)

    def send_all(pieces, like):
        first = Copy(*pieces[0])
        for piece in pieces[1:]:
            Copy(*piece, k=first.k)
        first.parts = like, like, first.parts[2]
        return first

    gone = [0]

    def flush(mark):
        for copy in sent[gone[0] : mark]:
            copy.wait_send()
        gone[0] = mark

    loads = []

    def load(source, target):
        copy = pltpu.make_async_copy(source, target, load_sems.at[len(loads)])
        copy.start()
        loads.append(copy)
        return copy

    x_load = load(x_ref, xin)
    small_in = (g1_ref, s1_ref, bo_ref, g2_ref, s2_ref, bd_ref, bq_ref, bv_ref, bu_ref)
    small_loads = [load(source, target) for source, target in zip(small_in, small_refs)]
    own_rows = rows(d * HALF, HALF)
    qkv_loads = [load(ref, full.at[own_rows]) for ref, full in ((wv_ref, wvf), (wk_ref, wkf), (wq_ref, wqf))]
    cot_load = load(cot_ref, cotin)
    ff_loads = [load(wu_ref, wuf.at[t, own_rows]), load(wd_ref, wdt.at[t, own_rows]), load(wo_ref, wof.at[t, d])]
    limit = count_ref[0]
    x_load.wait()
    tokens = jnp.concatenate([xin[0].astype(F32), jnp.zeros((PAD - OWN, WIDE), F32)], axis=0)
    kvx[c, chip_y] = tokens.astype(BF16)
    qx[chip_x] = tokens.astype(BF16)
    vec[t, d] = jnp.zeros((16, WIDE), F32)
    for i, (copy, ref, size) in enumerate(zip(small_loads, small_refs, SMALL)):
        copy.wait()
        vec[t, d, i : i + 1, 0:size] = jnp.reshape(ref[...].astype(F32), (1, size))

    pl.semaphore_wait(barrier, len(partners))

    def ring(view, places, devices):
        cuts = pl.ds(0, 80), pl.ds(80, 64)
        own, down, up, _ = places
        _, minus, plus, _ = devices
        going = {}

        def put(i, half, device):
            return send(lambda: view(i, cuts[half]), lambda: view(i, cuts[half]), device)

        def start():
            for half in range(2):
                for way, device in enumerate((plus, minus)):
                    going[half, way] = put(own, half, device)

        def near():
            for half in range(2):
                going[half, half].wait_recv()
                going["far", half] = put((down, up)[half], half, (plus, minus)[half])
            for half in range(2):
                going[half, 1 - half].wait_recv()

        def last():
            for half in range(2):
                going["far", half].wait_recv()

        return start, near, last

    kv_start, kv_near, kv_last = ring(lambda i, cut: kvx.at[c, i, cut], ys, y_dev)
    qx_start, qx_near, qx_last = ring(lambda i, cut: qx.at[i, cut], xs, x_dev)
    do_start, do_near, do_last = ring(lambda i, cut: dob.at[i, cut], xs, x_dev)

    def share(i):
        return send(lambda: kvx.at[c, i], lambda: kvx.at[c, i], sib)

    kv_start()
    shares = [share(ys[0])]
    qx_start()
    vec_copies = [send(vec.at[t, d], vec.at[t, d], device) for device in (z_dp, z_tensor, z_both)]
    part = rows(c * 96, 96)
    first = [
        (full, send(ref.at[part], full.at[rows(d * HALF + c * 96, 96)], z_dp))
        for ref, full in ((wv_ref, wvf), (wk_ref, wkf), (wq_ref, wqf))
    ]
    def at_part(full, to_t, to_d, first=0, size=96):
        if full is wof:
            return full.at[to_t, to_d, rows(c * 96 + first, size)]
        return full.at[to_t, rows(to_d * HALF + c * 96 + first, size)]

    def move(full, to_t, to_d, first, size, device):
        def view():
            return at_part(full, to_t, to_d, first, size)

        return send(view, view, device)

    out_copies = [send(wo_ref.at[part], at_part(wof, t, d), device) for device in (z_dp, z_both, z_tensor)]
    by_dp, by_both, relayed, handed = {}, {}, {}, {}
    for name, ref, full in (("up", wu_ref, wuf), ("down", wd_ref, wdt)):
        by_dp[name] = full, send(ref.at[part], at_part(full, t, d), z_dp)
        by_both[name] = full, send(ref.at[part], at_part(full, t, d), z_both)

    def hand_out():
        for copy in out_copies:
            copy.wait_recv()
        handed["out"] = [
            move(wof, to_t, to_d, 0, 96, sib) for to_t, to_d in ((t, d_other), (t_other, d_other), (t_other, d))
        ]

    def relay(name):
        full, copy = by_dp[name]
        copy.wait_recv()
        relayed[name] = [move(full, t, d_other, 0, 48, z_both)]
        handed[name] = [move(full, t, d_other, 0, 96, sib)]
        _, copy = by_both[name]
        copy.wait_recv()
        relayed[name].append(move(full, t_other, d_other, 48, 48, z_dp))
        handed[name, "far"] = [move(full, t_other, d_other, 0, 96, sib)]

    def hand_relayed(name):
        for copy in relayed[name]:
            copy.wait_recv()
        handed[name, "far"].append(move(by_dp[name][0], t_other, d, 0, 96, sib))

    def have(*names):
        for name in names:
            for copy in handed[name]:
                copy.wait_recv()

    center = tokens - jnp.mean(tokens, axis=1, keepdims=True)
    scale = lax.rsqrt(jnp.mean(center * center, axis=1, keepdims=True) + EPSILON)
    xh1[...] = center * scale
    rstd1[...] = scale
    row = lax.broadcasted_iota(jnp.int32, (PAD, 1), 0)
    own_ok = (row < OWN) & (n * OWN + row < limit)
    cot_load.wait()
    cot = jnp.concatenate([cotin[0].astype(F32), jnp.zeros((PAD - OWN, WIDE), F32)], axis=0)
    gout[...] = jnp.where(own_ok, cot, 0.0)
    for half, core in enumerate((c, 1 - c)):
        for y in range(4):
            where = (chip_x * 4 + y) * 2 + core
            ok = (row < OWN) & (where * OWN + row < limit)
            bias[half, pl.ds(y * PAD, PAD), :] = jnp.where(ok, 0.0, -1e30)

    def normed_of(tokens):
        ones = jnp.full((WIDE, 128), 1.0, BF16)
        mean = mm(tokens, ones) * (1.0 / WIDE)
        center = tokens.astype(F32) - jnp.concatenate([mean] * 3, axis=1)
        scale = lax.rsqrt(mm((center * center).astype(BF16), ones) * (1.0 / WIDE) + EPSILON)
        return (center * jnp.concatenate([scale] * 3, axis=1) * gain1 + shift1).astype(BF16)

    kv_near()
    shares += [share(ys[1]), share(ys[2])]
    qx_near()
    vec_copies[0].wait_recv()
    vfull[...] = vec[t, 0] + pltpu.roll(vec[t, 1], HALF, 1)
    bias_half = vec[t, 0] + pltpu.roll(vec[t, 1], 96, 1)
    gain1, shift1 = vfull[0:1, :], vfull[1:2, :]
    normed1 = (xh1[...] * gain1 + shift1).astype(BF16)
    n1[...] = normed1
    nkv[0, ys[0]] = normed1
    nq[xs[0]] = normed1
    for j in (1, 2):
        nkv[0, ys[j]] = normed_of(kvx[c, ys[j]])
        nq[xs[j]] = normed_of(qx[xs[j]])
    second = []
    for full, copy in first:
        copy.wait_recv()

        def half_of(full=full):
            return full.at[rows(d_other * HALF + c * 96, 96)]

        second.append(send(half_of, half_of, sib))
    for copy in qkv_loads:
        copy.wait()
    kv_last()
    shares.append(share(ys[3]))
    nkv[0, ys[3]] = normed_of(kvx[c, ys[3]])
    qx_last()
    nq[xs[3]] = normed_of(qx[xs[3]])
    for copy in second:
        copy.wait_recv()
    for i, full in enumerate((wkf, wvf, wqf)):
        wall[i] = widen(full[...].astype(F32)).astype(BF16)
    for i in range(2):
        wall_t[i] = jnp.transpose(widen((wkf, wvf)[i][...].astype(F32))).astype(BF16)
    lane = lanes_of((PAD, 256))
    tile_lane = lanes_of((PAD, 128))
    wide_lane = lanes_of((GROUP, 256))
    ones_v = jnp.where((lanes_of((1, 256)) >= HALF) & (lanes_of((1, 256)) < HALF + 9), 1.0, 0.0)
    bias_v = jnp.where(lanes_of((1, 256)) < HALF, bias_half[7:8, 0:256], 0.0)
    bias_q = jnp.where(lanes_of((1, 256)) < HALF, bias_half[6:7, 0:256], 0.0)
    bias_v_t = jnp.transpose(jnp.broadcast_to(bias_v + ones_v, (128, 256)))[:, 0:1]

    def head_lanes(h):
        return (lane >= 64 * h) & (lane < 64 + 64 * h)

    query = (mm(nq[...].reshape(GROUP, WIDE), wall[2]) + bias_q).astype(BF16)
    qall[...] = query.reshape(4, PAD, 256)
    for j in range(4):
        query = qall[xs[j]].astype(F32) * 0.125
        for h in range(3):
            qbig[j, pl.ds(h * PAD, PAD), :] = jnp.where(
                head_lanes(h), query, jnp.where(lane == HALF, 1.0, 0.0)
            ).astype(BF16)

    def project(half):
        normed = nkv[half].reshape(GROUP, WIDE)
        kbuf[pl.ds(half * GROUP, GROUP), :] = jnp.where(
            wide_lane == HALF, bias[half], mm(normed, wall[0])
        ).astype(BF16)
        vbuf[pl.ds(half * GROUP, GROUP), :] = (mm(normed, wall[1]) + (bias_v + ones_v)).astype(BF16)
        kt[half] = mm_nt(wall_t[0], normed).astype(BF16)
        vt[half] = (mm_nt(wall_t[1], normed) + bias_v_t).astype(BF16)

    project(0)
    for j in range(4):
        shares[j].wait_recv()
        nkv[1, ys[j]] = normed_of(kvx[1 - c, ys[j]])
    project(1)

    across = lanes_of((PAD, STACK)) - lax.broadcasted_iota(jnp.int32, (PAD, STACK), 0)
    picker[...] = jnp.where((across == 0) | (across == PAD) | (across == 2 * PAD), 1.0, 0.0).astype(BF16)

    def head_of_column(shape):
        column = lanes_of(shape)
        return (column >= PAD).astype(jnp.int32) + (column >= 2 * PAD).astype(jnp.int32)

    def own_head(value):
        down = lax.broadcasted_iota(jnp.int32, (HALF, STACK), 0)
        return jnp.where(((down >= 64).astype(jnp.int32) + (down >= 128).astype(jnp.int32)) == head_of_column((HALF, STACK)), value, 0.0)

    def parts_block(line):
        down = lax.broadcasted_iota(jnp.int32, (16, STACK), 0)
        head = (down >= 3).astype(jnp.int32) + (down >= 6).astype(jnp.int32)
        high, middle, rest = three_parts(line)
        i = down - 3 * head
        value = jnp.where(i == 0, high, jnp.where(i == 1, middle, rest))
        return jnp.where((head == head_of_column((16, STACK))) & (down < 9), value, 0.0)

    def times(left, right):
        return mm(left[0], right[0:GROUP]) + mm(left[1], right[GROUP:])

    def forward(j):
        scores = mm_nt(kbuf[...], qbig[j])
        top = jnp.max(scores, axis=0, keepdims=True)
        low = jnp.exp(scores - top).astype(BF16)
        pt[j] = low
        mrow[j] = top
        mixed = times([vt[i, 0:208, :] for i in range(2)], low)
        total = mixed[HALF : HALF + 1, :]
        whole = [own_head(mixed[0:HALF] * (1.0 / total)), parts_block(top), parts_block(total), jnp.zeros((32, STACK), F32)]
        om[j] = mm_nt(picker[...], jnp.concatenate(whole, axis=0).astype(BF16)).astype(BF16)

    partial = {}

    def send_partial(j):
        partial[j] = send(lambda: om.at[j], lambda: omr.at[j - 1], x_dev[j])

    @pl.loop(0, 4)
    def _(i):
        forward(3 - i)

        @pl.when(i == 0)
        def _():
            send_partial(3)
            hand_out()
            relay("up")

        @pl.when(i == 1)
        def _():
            send_partial(2)
            relay("down")

        @pl.when(i == 2)
        def _():
            send_partial(1)

    x_mark = len(sent)
    for j in (3, 2, 1):
        partial[j].wait_recv()
    messages = [om[0].astype(F32)] + [omr[j].astype(F32) for j in range(3)]
    tops, sums = [], []
    for message in messages:
        tile = message[:, 128:256]
        tile = tile + pltpu.roll(tile, 127, 1) + pltpu.roll(tile, 126, 1)
        tops.append(tile)
        sums.append(pltpu.roll(tile, 112, 1))
    top = jnp.maximum(jnp.maximum(tops[0], tops[1]), jnp.maximum(tops[2], tops[3]))
    parts = [jnp.exp(own - top) * total for own, total in zip(tops, sums)]
    total = parts[0] + parts[1] + parts[2] + parts[3]
    over = 1.0 / total
    lse = top + jnp.log(total)
    attended = jnp.zeros((PAD, 256), F32)
    for message, own in zip(messages, parts):
        ratio = own * over
        spread = jnp.where(lane < 64, ratio[:, 64:65], jnp.where(lane < 128, ratio[:, 67:68], ratio[:, 70:71]))
        attended = attended + message * spread
    attended = jnp.where(lane < HALF, attended, 0.0)
    attf[...] = attended
    attx[t] = attended[:, 0:HALF].astype(BF16)
    att_copy = send(attx.at[t], attx.at[t], z_tensor)
    hand_relayed("up")
    hand_relayed("down")
    have("out", "up", "down")
    for copy in ff_loads:
        copy.wait()
    for copy in vec_copies[1:]:
        copy.wait_recv()
    for i in range(2):
        woc[i] = jnp.concatenate([wof[i, 0], wof[i, 1]], axis=1)
    grad_low = gout[...].astype(BF16)
    valid = (tile_lane == 64) | (tile_lane == 67) | (tile_lane == 70)
    high, middle, rest = three_parts(jnp.where(valid, lse, 0.0))
    stats = pltpu.roll(high, 16, 1) + pltpu.roll(middle, 17, 1) + pltpu.roll(rest, 18, 1)
    flush(x_mark)
    att_copy.wait_recv()

    tokens = jnp.concatenate([xin[0].astype(F32), jnp.zeros((PAD - OWN, WIDE), F32)], axis=0)
    hidden1 = tokens + (mm(attx[0], woc[0]) + mm(attx[1], woc[1])) + vfull[2:3, :]
    hid[...] = hidden1
    center = hidden1 - jnp.mean(hidden1, axis=1, keepdims=True)
    scale = lax.rsqrt(jnp.mean(center * center, axis=1, keepdims=True) + EPSILON)
    xhat2 = center * scale
    xh2[...] = xhat2
    rstd2[...] = scale
    n2[...] = (xhat2 * vfull[3:4, :] + vfull[4:5, :]).astype(BF16)

    @pl.loop(0, 2)
    def _(step):
        i = t + step * (1 - 2 * t)

        @pl.when(step == 1)
        def _():
            have(("up", "far"), ("down", "far"))

        bias_up = jnp.concatenate([vec[i, 0, 8:9, :], vec[i, 1, 8:9, :]], axis=1)
        upper = mm(n2[...], wuf[i]) + bias_up
        gate = 0.5 + 0.5 * lax.erf(upper * 0.7071067811865476)
        act[i] = (upper * gate).astype(BF16)
        slope = gate + upper * jnp.exp(upper * upper * -0.5) * 0.3989422804014327
        gup[i] = (mm(grad_low, wdt[i]) * slope).astype(BF16)
        gn2p[i] = mm_nt(gup[i], wuf[i])

    grad_n2 = gn2p[0] + gn2p[1]

    xhat2 = xh2[...]
    z = grad_n2 * vfull[3:4, :]
    mean_z = jnp.mean(z, axis=1, keepdims=True)
    mean_zx = jnp.mean(z * xhat2, axis=1, keepdims=True)
    grad_h = gout[...] + (z - mean_z - xhat2 * mean_zx) * rstd2[...]
    ghid[...] = grad_h
    grad_h_low = grad_h.astype(BF16)
    grad_att = mm_nt(grad_h_low, woc[t]).astype(BF16)
    grad_att_w = widen(grad_att).astype(F32)
    product = grad_att_w * attf[...]
    message = jnp.where(tile_lane < 64, grad_att_w[:, 128:256], stats)
    for h in range(3):
        delta = jnp.sum(jnp.where(head_lanes(h), product, 0.0), axis=1, keepdims=True)
        for i, piece in enumerate(three_parts(delta)):
            message = jnp.where(tile_lane == 64 + 3 * h + i, -piece, message)
    dob[chip_x] = jnp.concatenate([grad_att_w[:, 0:128], message], axis=1).astype(BF16)
    do_start()
    def put_tiles(buf, dp, at, tall):
        r = tall.shape[0]
        buf[dp, pl.ds(at, r), :] = tall[:, 0:128].astype(BF16)
        tail = jnp.concatenate([tall[0 : r // 2, 128:HALF], tall[r // 2 :, 128:HALF]], axis=1)
        buf[dp, pl.ds(at + r, r // 2), :] = tail.astype(BF16)

    def put_rows(buf, at, pieces):
        for dp in range(2):
            lines = []
            for pair in pieces:
                line = pair[dp]
                size = line.shape[1]
                for i in range(0, size, 128):
                    piece = line[:, i : min(i + 128, size)]
                    if piece.shape[1] < 128:
                        piece = jnp.concatenate([piece, jnp.zeros((1, 128 - piece.shape[1]), F32)], axis=1)
                    lines.append(piece)
            lines.append(jnp.zeros((16 - len(lines), 128), F32))
            buf[dp, pl.ds(at, 16), :] = jnp.concatenate(lines, axis=0).astype(BF16)

    def halves(line):
        size = line.shape[1] // 2
        return line[:, 0:size], line[:, size:]

    def column_sum(value):
        return jnp.sum(value, axis=0, keepdims=True)

    def put_wide(buf, at, whole):
        for dp in range(2):
            for i in range(6):
                buf[dp, pl.ds(at + i * HALF, HALF), :] = whole[
                    dp * HALF : (dp + 1) * HALF, i * 128 : (i + 1) * 128
                ].astype(BF16)

    def reduction(r, src, from_sib, s0, from_a, s1, from_bz, fin):
        state = {}

        def to_sib():
            state["sib"] = [send(lambda: src.at[:, rows((1 - c) * 16 * r, 16 * r)], from_sib, sib)]

        def to_a():
            for copy in state["sib"]:
                copy.wait_recv()
            for dp in range(2):
                own = src[dp, rows(c * 16 * r, 16 * r), :].astype(F32)
                s0[dp] = (own + from_sib[dp].astype(F32)).astype(BF16)
            state["a"] = [
                send(lambda to=to: s0.at[:, rows(to * 4 * r, 4 * r)], lambda i=i: from_a.at[i], device)
                for i, (to, device) in enumerate(along_a)
            ]

        def to_bz():
            for copy in state["a"]:
                copy.wait_recv()
            for dp in range(2):
                summed = s0[dp, rows(a * 4 * r, 4 * r), :].astype(F32)
                for i in range(3):
                    summed = summed + from_a[i, dp].astype(F32)
                s1[dp] = summed.astype(BF16)
            state["b"] = [
                send(lambda to=to: s1.at[d, rows(to * r, r)], lambda i=i: from_bz.at[i], device)
                for i, (to, device) in enumerate(along_b)
            ]
            for i, (to, device) in enumerate(zip((b, b_up, b_far, b_down), other_plane)):
                state["b"].append(
                    send(lambda to=to: s1.at[d_other, rows(to * r, r)], lambda i=i: from_bz.at[3 + i], device)
                )

        def back_b():
            for copy in state["b"]:
                copy.wait_recv()
            summed = s1[d, rows(b * r, r), :].astype(F32)
            for i in range(7):
                summed = summed + from_bz[i].astype(F32)
            fin[rows(((c * 4 + a) * 4 + b) * r, r), :] = summed.astype(BF16)

            def place():
                return fin.at[rows(((c * 4 + a) * 4 + b) * r, r)]

            state["back_b"] = [send(place, place, device) for _, device in along_b]

        def back_a():
            for copy in state["back_b"]:
                copy.wait_recv()

            def place():
                return fin.at[rows((c * 4 + a) * 4 * r, 4 * r)]

            state["back_a"] = [send(place, place, device) for _, device in along_a]
            state["share"] = [send(place, place, sib)]

        def share():
            for copy, came in zip(state["back_a"], (a_down, a_far, a_up)):
                copy.wait_recv()

                def place(came=came):
                    return fin.at[rows((c * 4 + came) * 4 * r, 4 * r)]

                state["share"].append(send(place, place, sib))

        def end():
            for copy in state["share"]:
                copy.wait_recv()

        return to_sib, to_a, to_bz, back_b, back_a, share, end

    def direct_reduction(r, src, from_sib, s0, from_all, fin, extra):
        state = {}

        def to_sib():
            state["sib"] = [send(lambda: src.at[:, rows((1 - c) * 16 * r, 16 * r)], from_sib, sib)]
            if extra is not None:
                for i, device in enumerate((z_tensor, tensor_sib)):
                    state["sib"].append(
                        send(lambda: src.at[:, pl.ds(NORM_ROWS, 16)], lambda i=i: extra.at[i], device)
                    )

        def to_owner():
            for copy in state["sib"]:
                copy.wait_recv()
            for dp in range(2):
                own = src[dp, rows(c * 16 * r, 16 * r), :].astype(F32)
                s0[dp] = (own + from_sib[dp].astype(F32)).astype(BF16)
            if extra is not None:
                at = NORM_ROWS - 16 * r
                line = lax.broadcasted_iota(jnp.int32, (16, 128), 0)
                mine = (line >= 2) & (line < 6) & (c == 1)
                for dp in range(2):
                    own = src[dp, rows(c * 16 * r + at, 16), :].astype(F32)
                    own = own + from_sib[dp, pl.ds(at, 16), :].astype(F32)
                    more = extra[0, dp].astype(F32) + extra[1, dp].astype(F32)
                    s0[dp, pl.ds(at, 16), :] = (own + jnp.where(mine, more, 0.0)).astype(BF16)
            state["owner"] = send_all(
                [
                    (
                        lambda plane=plane, place=place: s0.at[(d, d_other)[plane], rows((place[0] * 4 + place[1]) * r, r)],
                        lambda i=i: from_all.at[i],
                        device,
                    )
                    for i, plane, place, device in everywhere
                ],
                lambda: from_all.at[pl.ds(1, 31)],
            )

        def back():
            state["owner"].wait_recv()
            summed = s0[d, rows((a * 4 + b) * r, r), :].astype(F32)
            for i in range(1, 32):
                summed = summed + from_all[i].astype(F32)
            fin[rows((c * 16 + a * 4 + b) * r, r), :] = summed.astype(BF16)

            def place():
                return fin.at[rows((c * 16 + a * 4 + b) * r, r)]

            state["back"] = send_all(
                [(place, place, device) for _, plane, _, device in everywhere if plane == 0],
                lambda: from_all.at[pl.ds(1, 15)],
            )

        def share():
            state["back"].wait_recv()

            def place():
                return fin.at[rows(c * 16 * r, 16 * r)]

            state["share"] = send(place, place, sib)

        def end():
            state["share"].wait_recv()

        return to_sib, to_owner, back, share, end

    r1 = reduction(UNITS_1, src1, sib1, s01, ar1, s11, br1, fin1)
    r2 = direct_reduction(UNITS_2, src2, sib2, s02, all2, fin2, tr2)
    r3 = direct_reduction(UNITS_3, src3, sib3, s03, all3, fin3, None)

    acck[...] = jnp.zeros(acck.shape, F32)
    accv[...] = jnp.zeros(accv.shape, F32)

    def backward_start(j):
        at = xs[j] if isinstance(j, int) else (chip_x + 3 * (j == 1).astype(jnp.int32) + (j == 2).astype(jnp.int32)) % 4
        grad = dob[at]
        for h in range(3):
            here = head_lanes(h)
            for first in (HALF, HALF + 16):
                here = here | ((lane >= first + 3 * h) & (lane < first + 3 * h + 3))
            dobig[pl.ds(h * PAD, PAD), :] = jnp.where(here, grad.astype(F32), 0.0).astype(BF16)
        select = lanes_of((16, 256))
        select = jnp.where((select >= HALF + 16) & (select < HALF + 25), 1.0, 0.0).astype(BF16)
        lse_row = mm_nt(select, dobig[...])[0:1, :]
        factor[...] = jnp.exp(mrow[j] - lse_row)

    def backward_half(j, half):
        part_h = pl.ds(half * GROUP, GROUP)
        probs = pt[j, part_h, :].astype(F32) * factor[...]
        grad_scores = (probs * mm_nt(vbuf[part_h, :], dobig[...])).astype(BF16)
        gscore[part_h, :] = grad_scores
        accv[part_h, :] += mm(probs.astype(BF16), dobig[...])
        acck[part_h, :] += mm(grad_scores, qbig[j])

    def backward_end(j):
        grad_q = times([kt[i, 0:HALF, :] for i in range(2)], gscore[...])
        grad_q = jnp.concatenate([own_head(grad_q), jnp.zeros((64, STACK), F32)], axis=0)
        dqm[j] = (mm_nt(picker[...], grad_q.astype(BF16)) * 0.125).astype(BF16)

    grad_parts = {}

    def send_grad(j):
        grad_parts[j] = send(lambda: dqm.at[j], lambda: dqr.at[j - 1], x_dev[j])

    @pl.loop(0, 3)
    def _(j):
        backward_start(j)
        backward_half(j, 1)
        backward_half(j, 0)
        backward_end(j)

        @pl.when(j == 0)
        def _():
            do_near()
            put_wide(src1, 0, mm_tn(grad_low, act[t]))
            put_wide(src1, 1152, mm_tn(n2[...], gup[t]))
            put_rows(src1, 2304, [halves(column_sum(gup[t].astype(F32))), halves(column_sum(gout[...]))])
            src1[:, pl.ds(2320, 240), :] = jnp.zeros((2, 240, 128), BF16)
            r1[0]()

        @pl.when(j == 1)
        def _():
            send_grad(1)

        @pl.when(j == 2)
        def _():
            send_grad(2)
            do_last()

    backward_start(3)
    backward_half(3, 1)
    both_grads = jnp.concatenate([acck[pl.ds(GROUP, GROUP), 0:HALF], accv[pl.ds(GROUP, GROUP), 0:HALF]], axis=1)
    gsib[...] = both_grads.astype(BF16).reshape(4, PAD, WIDE)
    sib_grads = send(gsib, gsibr, sib)
    backward_half(3, 0)
    backward_end(3)
    send_grad(3)
    mixed = mm_nt(act[0], wdt[0]) + mm_nt(act[1], wdt[1])
    yout[...] = (hid[...] + mixed + vfull[5:6, :])[0:OWN].astype(BF16)
    stores = [load(yout, y_ref)]
    both_grads = jnp.concatenate([acck[pl.ds(0, GROUP), 0:HALF], accv[pl.ds(0, GROUP), 0:HALF]], axis=1)
    r1[1]()
    sib_grads.wait_recv()
    gown[...] = both_grads.reshape(4, PAD, WIDE) + gsibr[...].astype(F32)
    gy[...] = gown[...].astype(BF16)
    y_grads = [send(lambda j=j: gy.at[ys[j]], lambda j=j: gyr.at[j - 1], y_dev[j]) for j in (3, 2, 1)]
    attended_low = attx[t]
    for dp in range(2):
        put_tiles(src3, dp, 0, mm_tn(attended_low, grad_h_low[:, dp * HALF : (dp + 1) * HALF]))
    put_rows(
        src3,
        288,
        [halves(column_sum(grad_h)), halves(column_sum(grad_n2 * xhat2)), halves(column_sum(grad_n2))],
    )
    src3[:, pl.ds(304, 208), :] = jnp.zeros((2, 208, 128), BF16)
    r3[0]()
    src2[:, pl.ds(880, 144), :] = jnp.zeros((2, 144, 128), BF16)
    for j in (1, 2, 3):
        grad_parts[j].wait_recv()
    grad_q = dqm[0].astype(F32) + dqr[0].astype(F32) + dqr[1].astype(F32) + dqr[2].astype(F32)
    grad_q = grad_q.astype(BF16)[:, 0:HALF]
    whole = mm_tn(n1[...], grad_q)
    for dp in range(2):
        put_tiles(src2, dp, 0, whole[dp * HALF : (dp + 1) * HALF])
    sum_q = column_sum(grad_q.astype(F32))
    gnq[...] = mm_nt(grad_q, wqf[...])
    r1[2]()
    r3[1]()
    for copy in y_grads:
        copy.wait_recv()
    both_grads = gown[chip_y] + gyr[0].astype(F32) + gyr[1].astype(F32) + gyr[2].astype(F32)
    both_grads = both_grads.astype(BF16)
    grad_k, grad_v = both_grads[:, 0:HALF], both_grads[:, HALF:WIDE]
    grad_n1 = gnq[...] + mm_nt(grad_k, wkf[...]) + mm_nt(grad_v, wvf[...])
    gn1x[t] = grad_n1.astype(BF16)
    gn1_copy = send(gn1x.at[t], gn1x.at[t], z_tensor)
    normed1 = n1[...]
    at = 288
    for grad in (grad_k, grad_v):
        whole = mm_tn(normed1, grad)
        for dp in range(2):
            put_tiles(src2, dp, at, whole[dp * HALF : (dp + 1) * HALF])
        at += 288
    put_rows(
        src2,
        NORM_ROWS,
        [
            halves(sum_q),
            halves(column_sum(grad_v.astype(F32))),
            halves(column_sum(grad_n1 * xh1[...])),
            halves(column_sum(grad_n1)),
        ],
    )
    late_mark = len(sent)
    r2[0]()
    r1[3]()
    r3[2]()
    r2[1]()
    r1[4]()
    gn1_copy.wait_recv()
    grad_n1 = gn1x[0].astype(F32) + gn1x[1].astype(F32)
    xhat1 = xh1[...]
    z = grad_n1 * vfull[0:1, :]
    mean_z = jnp.mean(z, axis=1, keepdims=True)
    mean_zx = jnp.mean(z * xhat1, axis=1, keepdims=True)
    gxout[...] = (ghid[...] + (z - mean_z - xhat1 * mean_zx) * rstd1[...])[0:OWN]
    stores.append(load(gxout, gx_ref))
    r3[3]()
    r2[2]()
    r1[5]()
    r3[4]()
    stores.append(load(fin3, f3_ref))
    flush(late_mark)
    r2[3]()
    r1[6]()
    stores.append(load(fin1, f1_ref))
    r2[4]()
    stores.append(load(fin2, f2_ref))
    flush(len(sent))
    for copy in stores:
        copy.wait()


def finish_kernel(y_ref, gx_ref, f1_hbm, f2_hbm, f3_hbm, *refs):
    outs, refs = refs[:17], refs[17:]
    (f1_ref, f2_ref, f3_ref, gx_in, y_in), kept, (in_sems, out_sems) = refs[:5], refs[5:20], refs[20:]
    o_g1, o_s1, o_wq, o_bq, o_wk, o_wv, o_bv, o_wo, o_bo, o_g2, o_s2, o_wu, o_bu, o_wd, o_bd = kept
    copies = [
        pltpu.make_async_copy(source, target, in_sems.at[i])
        for i, (source, target) in enumerate(
            ((f1_hbm, f1_ref), (f2_hbm, f2_ref), (gx_ref, gx_in.at[0]), (y_ref, y_in.at[0]), (f3_hbm, f3_ref))
        )
    ]
    for copy in copies:
        copy.start()
    stored = []

    def store(*values):
        for value in values:
            i = len(stored)
            target = outs[i_of[id(value)]]
            stored.append(pltpu.make_async_copy(value, target, out_sems.at[i]))
            stored[-1].start()

    i_of = {id(ref): i + 2 for i, ref in enumerate(kept)}
    i_of.update({id(y_in): 0, id(gx_in): 1})

    def take_tiles(ref, at, out):
        r = out.shape[0]
        out[:, 0:128] = ref[pl.ds(at, r), :].astype(F32)
        tail = ref[pl.ds(at + r, r // 2), :].astype(F32)
        out[pl.ds(0, r // 2), 128:HALF] = tail[:, 0:64]
        out[pl.ds(r // 2, r // 2), 128:HALF] = tail[:, 64:128]
        store(out)

    def take_rows(ref, at, outs):
        block = ref[pl.ds(at, 16), :].astype(F32)
        i = 0
        for out in outs:
            size = out.shape[0]
            for j in range(0, size, 128):
                width = min(128, size - j)
                out[pl.ds(j, width)] = jnp.reshape(block[i : i + 1, 0:width], (width,))
                i += 1
            store(out)

    copies[0].wait()
    for at, out in ((0, o_wd), (1152, o_wu)):
        for i in range(6):
            out[:, i * 128 : (i + 1) * 128] = f1_ref[pl.ds(at + i * HALF, HALF), :].astype(F32)
        store(out)
    copies[2].wait()
    store(gx_in)
    copies[3].wait()
    store(y_in)
    take_rows(f1_ref, 2304, [o_bu, o_bd])
    copies[4].wait()
    take_tiles(f3_ref, 0, o_wo)
    take_rows(f3_ref, 288, [o_bo, o_g2, o_s2])
    copies[1].wait()
    take_tiles(f2_ref, 0, o_wq)
    take_tiles(f2_ref, 288, o_wk)
    take_tiles(f2_ref, 576, o_wv)
    take_rows(f2_ref, NORM_ROWS, [o_bq, o_bv, o_g1, o_s1])
    for copy in stored:
        copy.wait()


def vm(*shape, dtype=F32):
    return pltpu.VMEM(shape, dtype)


def reduction_scratch(r, direct):
    steps = [vm(32, r, 128, dtype=BF16)] if direct else [
        vm(3, 2, 4 * r, 128, dtype=BF16),
        vm(2, 4 * r, 128, dtype=BF16),
        vm(7, r, 128, dtype=BF16),
    ]
    return [
        vm(2, 32 * r, 128, dtype=BF16),
        vm(2, 16 * r, 128, dtype=BF16),
        vm(2, 16 * r, 128, dtype=BF16),
        *steps,
        vm(32 * r, 128, dtype=BF16),
    ]


def on_device(*args):
    in_hbm = pl.BlockSpec(memory_space=pltpu.HBM)
    scratch = [
        pltpu.SemaphoreType.DMA((COPIES,)),
        pltpu.SemaphoreType.DMA((COPIES,)),
        pltpu.SemaphoreType.DMA((24,)),
        vm(WIDE, HALF, dtype=BF16),
        vm(WIDE, HALF, dtype=BF16),
        vm(WIDE, HALF, dtype=BF16),
        vm(2, 2, HALF, HALF, dtype=BF16),
        vm(2, WIDE, HID, dtype=BF16),
        vm(2, WIDE, HID, dtype=BF16),
        vm(2, HALF, WIDE, dtype=BF16),
        vm(2, 2, 16, WIDE),
        vm(16, WIDE),
        vm(1, OWN, WIDE, dtype=BF16),
        vm(1, OWN, WIDE, dtype=BF16),
        *[vm(size, dtype=BF16) for size in SMALL],
        vm(2, 4, PAD, WIDE, dtype=BF16),
        vm(4, PAD, WIDE, dtype=BF16),
        vm(2, 4, PAD, WIDE, dtype=BF16),
        vm(4, PAD, WIDE, dtype=BF16),
        vm(4, PAD, 256, dtype=BF16),
        vm(PAD, STACK, dtype=BF16),
        vm(3, WIDE, 256, dtype=BF16),
        vm(2, 256, WIDE, dtype=BF16),
        vm(4, PAD, 256, dtype=BF16),
        vm(4, STACK, 256, dtype=BF16),
        vm(2 * GROUP, 256, dtype=BF16),
        vm(2 * GROUP, 256, dtype=BF16),
        vm(2, 256, GROUP, dtype=BF16),
        vm(2, 256, GROUP, dtype=BF16),
        vm(2, GROUP, 1),
        vm(4, 2 * GROUP, STACK, dtype=BF16),
        vm(4, 1, STACK),
        vm(4, PAD, 256, dtype=BF16),
        vm(3, PAD, 256, dtype=BF16),
        vm(STACK, 256, dtype=BF16),
        vm(1, STACK),
        vm(2 * GROUP, STACK, dtype=BF16),
        vm(2 * GROUP, 256),
        vm(2 * GROUP, 256),
        vm(4, PAD, 256, dtype=BF16),
        vm(3, PAD, 256, dtype=BF16),
        vm(4, PAD, WIDE, dtype=BF16),
        vm(4, PAD, WIDE, dtype=BF16),
        vm(4, PAD, WIDE),
        vm(4, PAD, WIDE, dtype=BF16),
        vm(3, PAD, WIDE, dtype=BF16),
        vm(PAD, WIDE),
        vm(PAD, 1),
        vm(PAD, WIDE, dtype=BF16),
        vm(PAD, WIDE),
        vm(PAD, 256),
        vm(2, PAD, HALF, dtype=BF16),
        vm(PAD, WIDE),
        vm(PAD, WIDE),
        vm(PAD, 1),
        vm(PAD, WIDE, dtype=BF16),
        vm(2, PAD, HID, dtype=BF16),
        vm(2, PAD, HID, dtype=BF16),
        vm(2, PAD, WIDE),
        vm(2, PAD, WIDE, dtype=BF16),
        vm(PAD, WIDE),
        vm(PAD, WIDE),
        *reduction_scratch(UNITS_1, False),
        *reduction_scratch(UNITS_2, True),
        *reduction_scratch(UNITS_3, True),
        vm(2, 2, 16, 128, dtype=BF16),
        vm(OWN, WIDE, dtype=BF16),
        vm(OWN, WIDE),
    ]
    args = list(args)
    args[16] = args[16].T
    specs = [in_hbm] * len(args)
    specs[1] = pl.BlockSpec(memory_space=pltpu.SMEM)
    parts = pl.pallas_call(
        layer_kernel,
        out_shape=[
            jax.ShapeDtypeStruct((OWN, WIDE), BF16),
            jax.ShapeDtypeStruct((OWN, WIDE), F32),
            jax.ShapeDtypeStruct((32 * UNITS_1, 128), BF16),
            jax.ShapeDtypeStruct((32 * UNITS_2, 128), BF16),
            jax.ShapeDtypeStruct((32 * UNITS_3, 128), BF16),
        ],
        in_specs=specs,
        out_specs=[in_hbm] * 5,
        scratch_shapes=scratch,
        compiler_params=pltpu.CompilerParams(
            collective_id=0, has_side_effects=True, vmem_limit_bytes=VMEM_BYTES
        ),
        name="layer",
    )(*args)
    quarter = [
        ((1, OWN, WIDE), BF16), ((1, OWN, WIDE), F32), ((HALF,), F32), ((HALF,), F32), ((HALF, HALF), F32),
        ((96,), F32), ((HALF, HALF), F32), ((HALF, HALF), F32), ((96,), F32), ((HALF, HALF), F32), ((HALF,), F32),
        ((HALF,), F32), ((HALF,), F32), ((HALF, HID), F32), ((WIDE,), F32), ((HALF, HID), F32), ((HALF,), F32),
    ]
    results = list(
        pl.pallas_call(
            finish_kernel,
            out_shape=[jax.ShapeDtypeStruct(shape, dtype) for shape, dtype in quarter],
            in_specs=[in_hbm] * 5,
            out_specs=[in_hbm] * len(quarter),
            scratch_shapes=[
                vm(32 * UNITS_1, 128, dtype=BF16),
                vm(32 * UNITS_2, 128, dtype=BF16),
                vm(32 * UNITS_3, 128, dtype=BF16),
                vm(1, OWN, WIDE),
                vm(1, OWN, WIDE, dtype=BF16),
                *[vm(*shape, dtype=dtype) for shape, dtype in quarter[2:]],
                pltpu.SemaphoreType.DMA((5,)),
                pltpu.SemaphoreType.DMA((17,)),
            ],
            compiler_params=pltpu.CompilerParams(vmem_limit_bytes=VMEM_BYTES),
            name="finish",
        )(*parts)
    )
    results[15] = results[15].T
    return tuple(results)


def solution(mesh):
    wide, split, mixed = P("dp"), P("dp", "tensor"), P(("tensor", "dp"))
    tokens, crossed = P("dp", "ctx", None), P("tensor", "dp")
    return jax.shard_map(
        on_device,
        mesh=mesh,
        in_specs=(
            tokens, P("dp"), tokens, wide, wide, split, mixed, split, split, mixed, crossed, wide,
            wide, wide, split, mixed, crossed, wide,
        ),
        out_specs=(
            tokens, tokens, wide, wide, split, mixed, split, split, mixed, crossed, wide,
            wide, wide, split, mixed, crossed, wide,
        ),
        check_vma=False,
    )
```

```python
import jax
import jax.numpy as jnp
from jax import lax
from jax.experimental import pallas as pl
from jax.experimental.pallas import tpu as pltpu
from jax.sharding import PartitionSpec as P

F32 = jnp.float32
BF16 = jnp.bfloat16
MESH = pl.DeviceIdType.MESH

HEAD = 64
OWN = 136
PAD = 144
WIDE = 384
HALF = 192
HID = 768
GROUP = 4 * PAD
STACK = 3 * PAD
EPSILON = 1e-06
UNITS_1 = 80
UNITS_2 = 32
UNITS_3 = 16
NORM_ROWS = 864
COPIES = 288
VMEM_BYTES = 63 * 1024 * 1024
SMALL = (HALF, HALF, HALF, HALF, HALF, HALF, 96, 96, WIDE)


def mm(left, right):
    return lax.dot_general(left, right, (((1,), (0,)), ((), ())), preferred_element_type=F32)


def mm_nt(left, right):
    return lax.dot_general(left, right, (((1,), (1,)), ((), ())), preferred_element_type=F32)


def mm_tn(left, right):
    return lax.dot_general(left, right, (((0,), (0,)), ((), ())), preferred_element_type=F32)


def rows(start, size):
    return pl.ds(pl.multiple_of(start, 16), size)


def lanes_of(shape):
    return lax.broadcasted_iota(jnp.int32, shape, 1)


def widen(value):
    return jnp.concatenate([value, jnp.zeros((value.shape[0], 64), value.dtype)], axis=1)


def three_parts(value):
    high = value.astype(BF16).astype(F32)
    rest = value - high
    middle = rest.astype(BF16).astype(F32)
    return high, middle, (rest - middle).astype(BF16).astype(F32)


def layer_kernel(
    x_ref, count_ref, cot_ref, g1_ref, s1_ref, wq_ref, bq_ref, wk_ref, wv_ref, bv_ref, wo_ref, bo_ref,
    g2_ref, s2_ref, wu_ref, bu_ref, wd_ref, bd_ref,
    y_ref, gx_ref, f1_ref, f2_ref, f3_ref,
    send_sems, recv_sems, load_sems,
    wqf, wkf, wvf, wof, wuf, wdt, woc, vec, vfull, xin, cotin, *rest_refs
):
    small_refs, rest_refs = rest_refs[: len(SMALL)], rest_refs[len(SMALL) :]
    (
    kvx, qx, nkv, nq, dob, picker, wall, wall_t, qall, qbig, kbuf, vbuf, kt, vt, bias, pt, mrow, om, omr, dobig, factor, gscore, acck, accv, dqm, dqr,
    gsib, gsibr, gown, gy, gyr,
    xh1, rstd1, n1, gout, attf, attx, hid, xh2, rstd2, n2, act, gup, gn2p, gn1x, ghid, gnq,
    src1, sib1, s01, ar1, s11, br1, fin1,
    src2, sib2, s02, all2, fin2, src3, sib3, s03, all3, fin3, tr2, yout, gxout,
    ) = rest_refs
    d, n, t = lax.axis_index("dp"), lax.axis_index("ctx"), lax.axis_index("tensor")
    c, chip = n % 2, n // 2
    chip_x, chip_y = chip // 4, chip % 4
    a, b = chip_x * (1 - c) + chip_y * c, chip_y * (1 - c) + chip_x * c

    def dev(to_a, to_b):
        to_x, to_y = to_a * (1 - c) + to_b * c, to_b * (1 - c) + to_a * c
        return (d, (to_x * 4 + to_y) * 2 + c, t)

    d_other, t_other = 1 - d, 1 - t
    sib = (d, n + 1 - 2 * c, t)
    z_dp, z_tensor, z_both = (d_other, n, t), (d, n, t_other), (d_other, n, t_other)
    a_up, a_down, a_far = (a + 1) % 4, (a + 3) % 4, (a + 2) % 4
    b_up, b_down, b_far = (b + 1) % 4, (b + 3) % 4, (b + 2) % 4

    def by_place(to_x, to_y):
        return (d, (to_x * 4 + to_y) * 2 + c, t)

    xs = [chip_x, (chip_x + 3) % 4, (chip_x + 1) % 4, (chip_x + 2) % 4]
    ys = [chip_y, (chip_y + 3) % 4, (chip_y + 1) % 4, (chip_y + 2) % 4]
    x_dev, y_dev = [by_place(x, chip_y) for x in xs], [by_place(chip_x, y) for y in ys]

    barrier = pltpu.get_barrier_semaphore()
    a_plus, a_minus, b_plus, b_minus = dev(a_up, b), dev(a_down, b), dev(a, b_up), dev(a, b_down)
    a_across, b_across = dev(a_far, b), dev(a, b_far)
    along_a = ((a_up, a_plus), (a_far, a_across), (a_down, a_minus))
    along_b = ((b_up, b_plus), (b_far, b_across), (b_down, b_minus))
    other_plane = [(d_other, device[1], t) for device in (z_dp, b_plus, b_across, b_minus)]
    tensor_sib = (d, sib[1], t_other)
    everywhere = [
        (plane, place, (d, d_other)[plane], dev(place[0], place[1]))
        for plane in range(2)
        for place in [(to_a, to_b) for to_a in (a, a_up, a_far, a_down) for to_b in (b, b_up, b_far, b_down)]
    ][1:]
    everywhere = [(i + 1, plane, place, (to_d, device[1], t)) for i, (plane, place, to_d, device) in enumerate(everywhere)]
    partners = [sib, z_tensor, z_both, tensor_sib] + [device for _, _, _, device in everywhere]
    for partner in partners:
        pl.semaphore_signal(barrier, inc=1, device_id=partner, device_id_type=MESH)

    sent = []

    class Copy:
        def __init__(self, source, target, device, k=None):
            self.parts = source, target, device
            self.k = k
            if k is None:
                self.k = len(sent)
                sent.append(self)
            self.made().start()

        def made(self):
            source, target, device = (part() if callable(part) else part for part in self.parts)
            return pltpu.make_async_remote_copy(
                src_ref=source, dst_ref=target, send_sem=send_sems.at[self.k], recv_sem=recv_sems.at[self.k],
                device_id=device, device_id_type=MESH,
            )

        def wait_recv(self):
            self.made().wait_recv()

        def wait_send(self):
            self.made().wait_send()

    def send(source, target, device):
        return Copy(source, target, device)

    def send_all(pieces, like):
        first = Copy(*pieces[0])
        for piece in pieces[1:]:
            Copy(*piece, k=first.k)
        first.parts = like, like, first.parts[2]
        return first

    gone = [0]

    def flush(mark):
        for copy in sent[gone[0] : mark]:
            copy.wait_send()
        gone[0] = mark

    loads = []

    def load(source, target):
        copy = pltpu.make_async_copy(source, target, load_sems.at[len(loads)])
        copy.start()
        loads.append(copy)
        return copy

    x_load = load(x_ref, xin)
    small_in = (g1_ref, s1_ref, bo_ref, g2_ref, s2_ref, bd_ref, bq_ref, bv_ref, bu_ref)
    small_loads = [load(source, target) for source, target in zip(small_in, small_refs)]
    own_rows = rows(d * HALF, HALF)
    qkv_loads = [load(ref, full.at[own_rows]) for ref, full in ((wv_ref, wvf), (wk_ref, wkf), (wq_ref, wqf))]
    cot_load = load(cot_ref, cotin)
    ff_loads = [load(wu_ref, wuf.at[t, own_rows]), load(wd_ref, wdt.at[t, own_rows]), load(wo_ref, wof.at[t, d])]
    limit = count_ref[0]
    x_load.wait()
    tokens = jnp.concatenate([xin[0].astype(F32), jnp.zeros((PAD - OWN, WIDE), F32)], axis=0)
    kvx[c, chip_y] = tokens.astype(BF16)
    qx[chip_x] = tokens.astype(BF16)
    vec[t, d] = jnp.zeros((16, WIDE), F32)
    for i, (copy, ref, size) in enumerate(zip(small_loads, small_refs, SMALL)):
        copy.wait()
        vec[t, d, i : i + 1, 0:size] = jnp.reshape(ref[...].astype(F32), (1, size))

    pl.semaphore_wait(barrier, len(partners))

    def ring(view, places, devices):
        cuts = pl.ds(0, 80), pl.ds(80, 64)
        own, down, up, _ = places
        _, minus, plus, _ = devices
        going = {}

        def put(i, half, device):
            return send(lambda: view(i, cuts[half]), lambda: view(i, cuts[half]), device)

        def start():
            for half in range(2):
                for way, device in enumerate((plus, minus)):
                    going[half, way] = put(own, half, device)

        def near():
            for half in range(2):
                going[half, half].wait_recv()
                going["far", half] = put((down, up)[half], half, (plus, minus)[half])
            for half in range(2):
                going[half, 1 - half].wait_recv()

        def last():
            for half in range(2):
                going["far", half].wait_recv()

        return start, near, last

    kv_start, kv_near, kv_last = ring(lambda i, cut: kvx.at[c, i, cut], ys, y_dev)
    qx_start, qx_near, qx_last = ring(lambda i, cut: qx.at[i, cut], xs, x_dev)
    do_start, do_near, do_last = ring(lambda i, cut: dob.at[i, cut], xs, x_dev)

    def share(i):
        return send(lambda: kvx.at[c, i], lambda: kvx.at[c, i], sib)

    kv_start()
    shares = [share(ys[0])]
    qx_start()
    vec_copies = [send(vec.at[t, d], vec.at[t, d], device) for device in (z_dp, z_tensor, z_both)]
    part = rows(c * 96, 96)
    first = [
        (full, send(ref.at[part], full.at[rows(d * HALF + c * 96, 96)], z_dp))
        for ref, full in ((wv_ref, wvf), (wk_ref, wkf), (wq_ref, wqf))
    ]
    def at_part(full, to_t, to_d, first=0, size=96):
        if full is wof:
            return full.at[to_t, to_d, rows(c * 96 + first, size)]
        return full.at[to_t, rows(to_d * HALF + c * 96 + first, size)]

    def move(full, to_t, to_d, first, size, device):
        def view():
            return at_part(full, to_t, to_d, first, size)

        return send(view, view, device)

    out_copies = [send(wo_ref.at[part], at_part(wof, t, d), device) for device in (z_dp, z_both, z_tensor)]
    by_dp, by_both, relayed, handed = {}, {}, {}, {}
    for name, ref, full in (("up", wu_ref, wuf), ("down", wd_ref, wdt)):
        by_dp[name] = full, send(ref.at[part], at_part(full, t, d), z_dp)
        by_both[name] = full, send(ref.at[part], at_part(full, t, d), z_both)

    def hand_out():
        for copy in out_copies:
            copy.wait_recv()
        handed["out"] = [
            move(wof, to_t, to_d, 0, 96, sib) for to_t, to_d in ((t, d_other), (t_other, d_other), (t_other, d))
        ]

    def relay(name):
        full, copy = by_dp[name]
        copy.wait_recv()
        relayed[name] = [move(full, t, d_other, 0, 48, z_both)]
        handed[name] = [move(full, t, d_other, 0, 96, sib)]
        _, copy = by_both[name]
        copy.wait_recv()
        relayed[name].append(move(full, t_other, d_other, 48, 48, z_dp))
        handed[name, "far"] = [move(full, t_other, d_other, 0, 96, sib)]

    def hand_relayed(name):
        for copy in relayed[name]:
            copy.wait_recv()
        handed[name, "far"].append(move(by_dp[name][0], t_other, d, 0, 96, sib))

    def have(*names):
        for name in names:
            for copy in handed[name]:
                copy.wait_recv()

    center = tokens - jnp.mean(tokens, axis=1, keepdims=True)
    scale = lax.rsqrt(jnp.mean(center * center, axis=1, keepdims=True) + EPSILON)
    xh1[...] = center * scale
    rstd1[...] = scale
    row = lax.broadcasted_iota(jnp.int32, (PAD, 1), 0)
    own_ok = (row < OWN) & (n * OWN + row < limit)
    cot_load.wait()
    cot = jnp.concatenate([cotin[0].astype(F32), jnp.zeros((PAD - OWN, WIDE), F32)], axis=0)
    gout[...] = jnp.where(own_ok, cot, 0.0)
    for half, core in enumerate((c, 1 - c)):
        for y in range(4):
            where = (chip_x * 4 + y) * 2 + core
            ok = (row < OWN) & (where * OWN + row < limit)
            bias[half, pl.ds(y * PAD, PAD), :] = jnp.where(ok, 0.0, -1e30)

    def normed_of(tokens):
        ones = jnp.full((WIDE, 128), 1.0, BF16)
        mean = mm(tokens, ones) * (1.0 / WIDE)
        center = tokens.astype(F32) - jnp.concatenate([mean] * 3, axis=1)
        scale = lax.rsqrt(mm((center * center).astype(BF16), ones) * (1.0 / WIDE) + EPSILON)
        return (center * jnp.concatenate([scale] * 3, axis=1) * gain1 + shift1).astype(BF16)

    kv_near()
    shares += [share(ys[1]), share(ys[2])]
    qx_near()
    vec_copies[0].wait_recv()
    vfull[...] = vec[t, 0] + pltpu.roll(vec[t, 1], HALF, 1)
    bias_half = vec[t, 0] + pltpu.roll(vec[t, 1], 96, 1)
    gain1, shift1 = vfull[0:1, :], vfull[1:2, :]
    normed1 = (xh1[...] * gain1 + shift1).astype(BF16)
    n1[...] = normed1
    nkv[0, ys[0]] = normed1
    nq[xs[0]] = normed1
    for j in (1, 2):
        nkv[0, ys[j]] = normed_of(kvx[c, ys[j]])
        nq[xs[j]] = normed_of(qx[xs[j]])
    second = []
    for full, copy in first:
        copy.wait_recv()

        def half_of(full=full):
            return full.at[rows(d_other * HALF + c * 96, 96)]

        second.append(send(half_of, half_of, sib))
    for copy in qkv_loads:
        copy.wait()
    kv_last()
    shares.append(share(ys[3]))
    nkv[0, ys[3]] = normed_of(kvx[c, ys[3]])
    qx_last()
    nq[xs[3]] = normed_of(qx[xs[3]])
    for copy in second:
        copy.wait_recv()
    for i, full in enumerate((wkf, wvf, wqf)):
        wall[i] = widen(full[...].astype(F32)).astype(BF16)
    for i in range(2):
        wall_t[i] = jnp.transpose(widen((wkf, wvf)[i][...].astype(F32))).astype(BF16)
    lane = lanes_of((PAD, 256))
    tile_lane = lanes_of((PAD, 128))
    wide_lane = lanes_of((GROUP, 256))
    ones_v = jnp.where((lanes_of((1, 256)) >= HALF) & (lanes_of((1, 256)) < HALF + 9), 1.0, 0.0)
    bias_v = jnp.where(lanes_of((1, 256)) < HALF, bias_half[7:8, 0:256], 0.0)
    bias_q = jnp.where(lanes_of((1, 256)) < HALF, bias_half[6:7, 0:256], 0.0)
    bias_v_t = jnp.transpose(jnp.broadcast_to(bias_v + ones_v, (128, 256)))[:, 0:1]

    def head_lanes(h):
        return (lane >= 64 * h) & (lane < 64 + 64 * h)

    query = (mm(nq[...].reshape(GROUP, WIDE), wall[2]) + bias_q).astype(BF16)
    qall[...] = query.reshape(4, PAD, 256)
    for j in range(4):
        query = qall[xs[j]].astype(F32) * 0.125
        for h in range(3):
            qbig[j, pl.ds(h * PAD, PAD), :] = jnp.where(
                head_lanes(h), query, jnp.where(lane == HALF, 1.0, 0.0)
            ).astype(BF16)

    def project(half):
        normed = nkv[half].reshape(GROUP, WIDE)
        kbuf[pl.ds(half * GROUP, GROUP), :] = jnp.where(
            wide_lane == HALF, bias[half], mm(normed, wall[0])
        ).astype(BF16)
        vbuf[pl.ds(half * GROUP, GROUP), :] = (mm(normed, wall[1]) + (bias_v + ones_v)).astype(BF16)
        kt[half] = mm_nt(wall_t[0], normed).astype(BF16)
        vt[half] = (mm_nt(wall_t[1], normed) + bias_v_t).astype(BF16)

    project(0)
    for j in range(4):
        shares[j].wait_recv()
        nkv[1, ys[j]] = normed_of(kvx[1 - c, ys[j]])
    project(1)

    across = lanes_of((PAD, STACK)) - lax.broadcasted_iota(jnp.int32, (PAD, STACK), 0)
    picker[...] = jnp.where((across == 0) | (across == PAD) | (across == 2 * PAD), 1.0, 0.0).astype(BF16)

    def head_of_column(shape):
        column = lanes_of(shape)
        return (column >= PAD).astype(jnp.int32) + (column >= 2 * PAD).astype(jnp.int32)

    def own_head(value):
        down = lax.broadcasted_iota(jnp.int32, (HALF, STACK), 0)
        return jnp.where(((down >= 64).astype(jnp.int32) + (down >= 128).astype(jnp.int32)) == head_of_column((HALF, STACK)), value, 0.0)

    def parts_block(line):
        down = lax.broadcasted_iota(jnp.int32, (16, STACK), 0)
        head = (down >= 3).astype(jnp.int32) + (down >= 6).astype(jnp.int32)
        high, middle, rest = three_parts(line)
        i = down - 3 * head
        value = jnp.where(i == 0, high, jnp.where(i == 1, middle, rest))
        return jnp.where((head == head_of_column((16, STACK))) & (down < 9), value, 0.0)

    def times(left, right):
        return mm(left[0], right[0:GROUP]) + mm(left[1], right[GROUP:])

    def forward(j):
        scores = mm_nt(kbuf[...], qbig[j])
        top = jnp.max(scores, axis=0, keepdims=True)
        low = jnp.exp(scores - top).astype(BF16)
        pt[j] = low
        mrow[j] = top
        mixed = times([vt[i, 0:208, :] for i in range(2)], low)
        total = mixed[HALF : HALF + 1, :]
        whole = [own_head(mixed[0:HALF] * (1.0 / total)), parts_block(top), parts_block(total), jnp.zeros((32, STACK), F32)]
        om[j] = mm_nt(picker[...], jnp.concatenate(whole, axis=0).astype(BF16)).astype(BF16)

    partial = {}

    def send_partial(j):
        partial[j] = send(lambda: om.at[j], lambda: omr.at[j - 1], x_dev[j])

    forward(3)
    send_partial(3)
    hand_out()
    relay("up")
    forward(2)
    send_partial(2)
    relay("down")
    forward(1)
    send_partial(1)
    forward(0)

    x_mark = len(sent)
    for j in (3, 2, 1):
        partial[j].wait_recv()
    messages = [om[0].astype(F32)] + [omr[j].astype(F32) for j in range(3)]
    tops, sums = [], []
    for message in messages:
        tile = message[:, 128:256]
        tile = tile + pltpu.roll(tile, 127, 1) + pltpu.roll(tile, 126, 1)
        tops.append(tile)
        sums.append(pltpu.roll(tile, 112, 1))
    top = jnp.maximum(jnp.maximum(tops[0], tops[1]), jnp.maximum(tops[2], tops[3]))
    parts = [jnp.exp(own - top) * total for own, total in zip(tops, sums)]
    total = parts[0] + parts[1] + parts[2] + parts[3]
    over = 1.0 / total
    lse = top + jnp.log(total)
    attended = jnp.zeros((PAD, 256), F32)
    for message, own in zip(messages, parts):
        ratio = own * over
        spread = jnp.where(lane < 64, ratio[:, 64:65], jnp.where(lane < 128, ratio[:, 67:68], ratio[:, 70:71]))
        attended = attended + message * spread
    attended = jnp.where(lane < HALF, attended, 0.0)
    attf[...] = attended
    attx[t] = attended[:, 0:HALF].astype(BF16)
    att_copy = send(attx.at[t], attx.at[t], z_tensor)
    hand_relayed("up")
    hand_relayed("down")
    have("out", "up", "down")
    for copy in ff_loads:
        copy.wait()
    for copy in vec_copies[1:]:
        copy.wait_recv()
    for i in range(2):
        woc[i] = jnp.concatenate([wof[i, 0], wof[i, 1]], axis=1)
    grad_low = gout[...].astype(BF16)
    valid = (tile_lane == 64) | (tile_lane == 67) | (tile_lane == 70)
    high, middle, rest = three_parts(jnp.where(valid, lse, 0.0))
    stats = pltpu.roll(high, 16, 1) + pltpu.roll(middle, 17, 1) + pltpu.roll(rest, 18, 1)
    flush(x_mark)
    att_copy.wait_recv()

    tokens = jnp.concatenate([xin[0].astype(F32), jnp.zeros((PAD - OWN, WIDE), F32)], axis=0)
    hidden1 = tokens + (mm(attx[0], woc[0]) + mm(attx[1], woc[1])) + vfull[2:3, :]
    hid[...] = hidden1
    center = hidden1 - jnp.mean(hidden1, axis=1, keepdims=True)
    scale = lax.rsqrt(jnp.mean(center * center, axis=1, keepdims=True) + EPSILON)
    xhat2 = center * scale
    xh2[...] = xhat2
    rstd2[...] = scale
    n2[...] = (xhat2 * vfull[3:4, :] + vfull[4:5, :]).astype(BF16)

    @pl.loop(0, 2)
    def _(step):
        i = t + step * (1 - 2 * t)

        @pl.when(step == 1)
        def _():
            have(("up", "far"), ("down", "far"))

        bias_up = jnp.concatenate([vec[i, 0, 8:9, :], vec[i, 1, 8:9, :]], axis=1)
        upper = mm(n2[...], wuf[i]) + bias_up
        gate = 0.5 + 0.5 * lax.erf(upper * 0.7071067811865476)
        act[i] = (upper * gate).astype(BF16)
        slope = gate + upper * jnp.exp(upper * upper * -0.5) * 0.3989422804014327
        gup[i] = (mm(grad_low, wdt[i]) * slope).astype(BF16)
        gn2p[i] = mm_nt(gup[i], wuf[i])

    grad_n2 = gn2p[0] + gn2p[1]

    xhat2 = xh2[...]
    z = grad_n2 * vfull[3:4, :]
    mean_z = jnp.mean(z, axis=1, keepdims=True)
    mean_zx = jnp.mean(z * xhat2, axis=1, keepdims=True)
    grad_h = gout[...] + (z - mean_z - xhat2 * mean_zx) * rstd2[...]
    ghid[...] = grad_h
    grad_h_low = grad_h.astype(BF16)
    grad_att = mm_nt(grad_h_low, woc[t]).astype(BF16)
    grad_att_w = widen(grad_att).astype(F32)
    product = grad_att_w * attf[...]
    message = jnp.where(tile_lane < 64, grad_att_w[:, 128:256], stats)
    for h in range(3):
        delta = jnp.sum(jnp.where(head_lanes(h), product, 0.0), axis=1, keepdims=True)
        for i, piece in enumerate(three_parts(delta)):
            message = jnp.where(tile_lane == 64 + 3 * h + i, -piece, message)
    dob[chip_x] = jnp.concatenate([grad_att_w[:, 0:128], message], axis=1).astype(BF16)
    do_start()
    def put_tiles(buf, dp, at, tall):
        r = tall.shape[0]
        buf[dp, pl.ds(at, r), :] = tall[:, 0:128].astype(BF16)
        tail = jnp.concatenate([tall[0 : r // 2, 128:HALF], tall[r // 2 :, 128:HALF]], axis=1)
        buf[dp, pl.ds(at + r, r // 2), :] = tail.astype(BF16)

    def put_rows(buf, at, pieces):
        for dp in range(2):
            lines = []
            for pair in pieces:
                line = pair[dp]
                size = line.shape[1]
                for i in range(0, size, 128):
                    piece = line[:, i : min(i + 128, size)]
                    if piece.shape[1] < 128:
                        piece = jnp.concatenate([piece, jnp.zeros((1, 128 - piece.shape[1]), F32)], axis=1)
                    lines.append(piece)
            lines.append(jnp.zeros((16 - len(lines), 128), F32))
            buf[dp, pl.ds(at, 16), :] = jnp.concatenate(lines, axis=0).astype(BF16)

    def halves(line):
        size = line.shape[1] // 2
        return line[:, 0:size], line[:, size:]

    def column_sum(value):
        return jnp.sum(value, axis=0, keepdims=True)

    def put_wide(buf, at, whole):
        for dp in range(2):
            for i in range(6):
                buf[dp, pl.ds(at + i * HALF, HALF), :] = whole[
                    dp * HALF : (dp + 1) * HALF, i * 128 : (i + 1) * 128
                ].astype(BF16)

    def reduction(r, src, from_sib, s0, from_a, s1, from_bz, fin):
        state = {}

        def to_sib():
            state["sib"] = [send(lambda: src.at[:, rows((1 - c) * 16 * r, 16 * r)], from_sib, sib)]

        def to_a():
            for copy in state["sib"]:
                copy.wait_recv()
            for dp in range(2):
                own = src[dp, rows(c * 16 * r, 16 * r), :].astype(F32)
                s0[dp] = (own + from_sib[dp].astype(F32)).astype(BF16)
            state["a"] = [
                send(lambda to=to: s0.at[:, rows(to * 4 * r, 4 * r)], lambda i=i: from_a.at[i], device)
                for i, (to, device) in enumerate(along_a)
            ]

        def to_bz():
            for copy in state["a"]:
                copy.wait_recv()
            for dp in range(2):
                summed = s0[dp, rows(a * 4 * r, 4 * r), :].astype(F32)
                for i in range(3):
                    summed = summed + from_a[i, dp].astype(F32)
                s1[dp] = summed.astype(BF16)
            state["b"] = [
                send(lambda to=to: s1.at[d, rows(to * r, r)], lambda i=i: from_bz.at[i], device)
                for i, (to, device) in enumerate(along_b)
            ]
            for i, (to, device) in enumerate(zip((b, b_up, b_far, b_down), other_plane)):
                state["b"].append(
                    send(lambda to=to: s1.at[d_other, rows(to * r, r)], lambda i=i: from_bz.at[3 + i], device)
                )

        def back_b():
            for copy in state["b"]:
                copy.wait_recv()
            summed = s1[d, rows(b * r, r), :].astype(F32)
            for i in range(7):
                summed = summed + from_bz[i].astype(F32)
            fin[rows(((c * 4 + a) * 4 + b) * r, r), :] = summed.astype(BF16)

            def place():
                return fin.at[rows(((c * 4 + a) * 4 + b) * r, r)]

            state["back_b"] = [send(place, place, device) for _, device in along_b]

        def back_a():
            for copy in state["back_b"]:
                copy.wait_recv()

            def place():
                return fin.at[rows((c * 4 + a) * 4 * r, 4 * r)]

            state["back_a"] = [send(place, place, device) for _, device in along_a]
            state["share"] = [send(place, place, sib)]

        def share():
            for copy, came in zip(state["back_a"], (a_down, a_far, a_up)):
                copy.wait_recv()

                def place(came=came):
                    return fin.at[rows((c * 4 + came) * 4 * r, 4 * r)]

                state["share"].append(send(place, place, sib))

        def end():
            for copy in state["share"]:
                copy.wait_recv()

        return to_sib, to_a, to_bz, back_b, back_a, share, end

    def direct_reduction(r, src, from_sib, s0, from_all, fin, extra):
        state = {}

        def to_sib():
            state["sib"] = [send(lambda: src.at[:, rows((1 - c) * 16 * r, 16 * r)], from_sib, sib)]
            if extra is not None:
                for i, device in enumerate((z_tensor, tensor_sib)):
                    state["sib"].append(
                        send(lambda: src.at[:, pl.ds(NORM_ROWS, 16)], lambda i=i: extra.at[i], device)
                    )

        def to_owner():
            for copy in state["sib"]:
                copy.wait_recv()
            for dp in range(2):
                own = src[dp, rows(c * 16 * r, 16 * r), :].astype(F32)
                s0[dp] = (own + from_sib[dp].astype(F32)).astype(BF16)
            if extra is not None:
                at = NORM_ROWS - 16 * r
                line = lax.broadcasted_iota(jnp.int32, (16, 128), 0)
                mine = (line >= 2) & (line < 6) & (c == 1)
                for dp in range(2):
                    own = src[dp, rows(c * 16 * r + at, 16), :].astype(F32)
                    own = own + from_sib[dp, pl.ds(at, 16), :].astype(F32)
                    more = extra[0, dp].astype(F32) + extra[1, dp].astype(F32)
                    s0[dp, pl.ds(at, 16), :] = (own + jnp.where(mine, more, 0.0)).astype(BF16)
            state["owner"] = send_all(
                [
                    (
                        lambda plane=plane, place=place: s0.at[(d, d_other)[plane], rows((place[0] * 4 + place[1]) * r, r)],
                        lambda i=i: from_all.at[i],
                        device,
                    )
                    for i, plane, place, device in everywhere
                ],
                lambda: from_all.at[pl.ds(1, 31)],
            )

        def back():
            state["owner"].wait_recv()
            summed = s0[d, rows((a * 4 + b) * r, r), :].astype(F32)
            for i in range(1, 32):
                summed = summed + from_all[i].astype(F32)
            fin[rows((c * 16 + a * 4 + b) * r, r), :] = summed.astype(BF16)

            def place():
                return fin.at[rows((c * 16 + a * 4 + b) * r, r)]

            state["back"] = send_all(
                [(place, place, device) for _, plane, _, device in everywhere if plane == 0],
                lambda: from_all.at[pl.ds(1, 15)],
            )

        def share():
            state["back"].wait_recv()

            def place():
                return fin.at[rows(c * 16 * r, 16 * r)]

            state["share"] = send(place, place, sib)

        def end():
            state["share"].wait_recv()

        return to_sib, to_owner, back, share, end

    r1 = reduction(UNITS_1, src1, sib1, s01, ar1, s11, br1, fin1)
    r2 = direct_reduction(UNITS_2, src2, sib2, s02, all2, fin2, tr2)
    r3 = direct_reduction(UNITS_3, src3, sib3, s03, all3, fin3, None)

    acck[...] = jnp.zeros(acck.shape, F32)
    accv[...] = jnp.zeros(accv.shape, F32)

    def backward_start(j):
        at = xs[j] if isinstance(j, int) else (chip_x + 3 * (j == 1).astype(jnp.int32) + (j == 2).astype(jnp.int32)) % 4
        grad = dob[at]
        for h in range(3):
            here = head_lanes(h)
            for first in (HALF, HALF + 16):
                here = here | ((lane >= first + 3 * h) & (lane < first + 3 * h + 3))
            dobig[pl.ds(h * PAD, PAD), :] = jnp.where(here, grad.astype(F32), 0.0).astype(BF16)
        select = lanes_of((16, 256))
        select = jnp.where((select >= HALF + 16) & (select < HALF + 25), 1.0, 0.0).astype(BF16)
        lse_row = mm_nt(select, dobig[...])[0:1, :]
        factor[...] = jnp.exp(mrow[j] - lse_row)

    def backward_half(j, half):
        part_h = pl.ds(half * GROUP, GROUP)
        probs = pt[j, part_h, :].astype(F32) * factor[...]
        grad_scores = (probs * mm_nt(vbuf[part_h, :], dobig[...])).astype(BF16)
        gscore[part_h, :] = grad_scores
        accv[part_h, :] += mm(probs.astype(BF16), dobig[...])
        acck[part_h, :] += mm(grad_scores, qbig[j])

    def backward_end(j):
        grad_q = times([kt[i, 0:HALF, :] for i in range(2)], gscore[...])
        grad_q = jnp.concatenate([own_head(grad_q), jnp.zeros((64, STACK), F32)], axis=0)
        dqm[j] = (mm_nt(picker[...], grad_q.astype(BF16)) * 0.125).astype(BF16)

    grad_parts = {}

    def send_grad(j):
        grad_parts[j] = send(lambda: dqm.at[j], lambda: dqr.at[j - 1], x_dev[j])

    def backward(j):
        backward_start(j)
        backward_half(j, 1)
        backward_half(j, 0)
        backward_end(j)

    backward(0)
    do_near()
    put_wide(src1, 0, mm_tn(grad_low, act[t]))
    put_wide(src1, 1152, mm_tn(n2[...], gup[t]))
    put_rows(src1, 2304, [halves(column_sum(gup[t].astype(F32))), halves(column_sum(gout[...]))])
    src1[:, pl.ds(2320, 240), :] = jnp.zeros((2, 240, 128), BF16)
    r1[0]()
    backward(1)
    send_grad(1)
    backward(2)
    send_grad(2)
    do_last()
    backward_start(3)
    backward_half(3, 1)
    both_grads = jnp.concatenate([acck[pl.ds(GROUP, GROUP), 0:HALF], accv[pl.ds(GROUP, GROUP), 0:HALF]], axis=1)
    gsib[...] = both_grads.astype(BF16).reshape(4, PAD, WIDE)
    sib_grads = send(gsib, gsibr, sib)
    backward_half(3, 0)
    backward_end(3)
    send_grad(3)
    mixed = mm_nt(act[0], wdt[0]) + mm_nt(act[1], wdt[1])
    yout[...] = (hid[...] + mixed + vfull[5:6, :])[0:OWN].astype(BF16)
    stores = [load(yout, y_ref)]
    both_grads = jnp.concatenate([acck[pl.ds(0, GROUP), 0:HALF], accv[pl.ds(0, GROUP), 0:HALF]], axis=1)
    r1[1]()
    sib_grads.wait_recv()
    gown[...] = both_grads.reshape(4, PAD, WIDE) + gsibr[...].astype(F32)
    gy[...] = gown[...].astype(BF16)
    y_grads = [send(lambda j=j: gy.at[ys[j]], lambda j=j: gyr.at[j - 1], y_dev[j]) for j in (3, 2, 1)]
    attended_low = attx[t]
    for dp in range(2):
        put_tiles(src3, dp, 0, mm_tn(attended_low, grad_h_low[:, dp * HALF : (dp + 1) * HALF]))
    put_rows(
        src3,
        288,
        [halves(column_sum(grad_h)), halves(column_sum(grad_n2 * xhat2)), halves(column_sum(grad_n2))],
    )
    src3[:, pl.ds(304, 208), :] = jnp.zeros((2, 208, 128), BF16)
    r3[0]()
    src2[:, pl.ds(880, 144), :] = jnp.zeros((2, 144, 128), BF16)
    for j in (1, 2, 3):
        grad_parts[j].wait_recv()
    grad_q = dqm[0].astype(F32) + dqr[0].astype(F32) + dqr[1].astype(F32) + dqr[2].astype(F32)
    grad_q = grad_q.astype(BF16)[:, 0:HALF]
    whole = mm_tn(n1[...], grad_q)
    for dp in range(2):
        put_tiles(src2, dp, 0, whole[dp * HALF : (dp + 1) * HALF])
    sum_q = column_sum(grad_q.astype(F32))
    gnq[...] = mm_nt(grad_q, wqf[...])
    r1[2]()
    r3[1]()
    for copy in y_grads:
        copy.wait_recv()
    both_grads = gown[chip_y] + gyr[0].astype(F32) + gyr[1].astype(F32) + gyr[2].astype(F32)
    both_grads = both_grads.astype(BF16)
    grad_k, grad_v = both_grads[:, 0:HALF], both_grads[:, HALF:WIDE]
    grad_n1 = gnq[...] + mm_nt(grad_k, wkf[...]) + mm_nt(grad_v, wvf[...])
    gn1x[t] = grad_n1.astype(BF16)
    gn1_copy = send(gn1x.at[t], gn1x.at[t], z_tensor)
    normed1 = n1[...]
    at = 288
    for grad in (grad_k, grad_v):
        whole = mm_tn(normed1, grad)
        for dp in range(2):
            put_tiles(src2, dp, at, whole[dp * HALF : (dp + 1) * HALF])
        at += 288
    put_rows(
        src2,
        NORM_ROWS,
        [
            halves(sum_q),
            halves(column_sum(grad_v.astype(F32))),
            halves(column_sum(grad_n1 * xh1[...])),
            halves(column_sum(grad_n1)),
        ],
    )
    late_mark = len(sent)
    r2[0]()
    r1[3]()
    r3[2]()
    r2[1]()
    r1[4]()
    gn1_copy.wait_recv()
    grad_n1 = gn1x[0].astype(F32) + gn1x[1].astype(F32)
    xhat1 = xh1[...]
    z = grad_n1 * vfull[0:1, :]
    mean_z = jnp.mean(z, axis=1, keepdims=True)
    mean_zx = jnp.mean(z * xhat1, axis=1, keepdims=True)
    gxout[...] = (ghid[...] + (z - mean_z - xhat1 * mean_zx) * rstd1[...])[0:OWN]
    stores.append(load(gxout, gx_ref))
    r3[3]()
    r2[2]()
    r1[5]()
    r3[4]()
    stores.append(load(fin3, f3_ref))
    flush(late_mark)
    r2[3]()
    r1[6]()
    stores.append(load(fin1, f1_ref))
    r2[4]()
    stores.append(load(fin2, f2_ref))
    flush(len(sent))
    for copy in stores:
        copy.wait()


def finish_kernel(y_ref, gx_ref, f1_hbm, f2_hbm, f3_hbm, *refs):
    outs, refs = refs[:17], refs[17:]
    (f1_ref, f2_ref, f3_ref, gx_in, y_in), kept, (in_sems, out_sems) = refs[:5], refs[5:20], refs[20:]
    o_g1, o_s1, o_wq, o_bq, o_wk, o_wv, o_bv, o_wo, o_bo, o_g2, o_s2, o_wu, o_bu, o_wd, o_bd = kept
    copies = [
        pltpu.make_async_copy(source, target, in_sems.at[i])
        for i, (source, target) in enumerate(
            ((f1_hbm, f1_ref), (f2_hbm, f2_ref), (gx_ref, gx_in.at[0]), (y_ref, y_in.at[0]), (f3_hbm, f3_ref))
        )
    ]
    for copy in copies:
        copy.start()
    stored = []

    def store(*values):
        for value in values:
            i = len(stored)
            target = outs[i_of[id(value)]]
            stored.append(pltpu.make_async_copy(value, target, out_sems.at[i]))
            stored[-1].start()

    i_of = {id(ref): i + 2 for i, ref in enumerate(kept)}
    i_of.update({id(y_in): 0, id(gx_in): 1})

    def take_tiles(ref, at, out):
        r = out.shape[0]
        out[:, 0:128] = ref[pl.ds(at, r), :].astype(F32)
        tail = ref[pl.ds(at + r, r // 2), :].astype(F32)
        out[pl.ds(0, r // 2), 128:HALF] = tail[:, 0:64]
        out[pl.ds(r // 2, r // 2), 128:HALF] = tail[:, 64:128]
        store(out)

    def take_rows(ref, at, outs):
        block = ref[pl.ds(at, 16), :].astype(F32)
        i = 0
        for out in outs:
            size = out.shape[0]
            for j in range(0, size, 128):
                width = min(128, size - j)
                out[pl.ds(j, width)] = jnp.reshape(block[i : i + 1, 0:width], (width,))
                i += 1
            store(out)

    copies[0].wait()
    for at, out in ((0, o_wd), (1152, o_wu)):
        for i in range(6):
            out[:, i * 128 : (i + 1) * 128] = f1_ref[pl.ds(at + i * HALF, HALF), :].astype(F32)
        store(out)
    copies[2].wait()
    store(gx_in)
    copies[3].wait()
    store(y_in)
    take_rows(f1_ref, 2304, [o_bu, o_bd])
    copies[4].wait()
    take_tiles(f3_ref, 0, o_wo)
    take_rows(f3_ref, 288, [o_bo, o_g2, o_s2])
    copies[1].wait()
    take_tiles(f2_ref, 0, o_wq)
    take_tiles(f2_ref, 288, o_wk)
    take_tiles(f2_ref, 576, o_wv)
    take_rows(f2_ref, NORM_ROWS, [o_bq, o_bv, o_g1, o_s1])
    for copy in stored:
        copy.wait()


def vm(*shape, dtype=F32):
    return pltpu.VMEM(shape, dtype)


def reduction_scratch(r, direct):
    steps = [vm(32, r, 128, dtype=BF16)] if direct else [
        vm(3, 2, 4 * r, 128, dtype=BF16),
        vm(2, 4 * r, 128, dtype=BF16),
        vm(7, r, 128, dtype=BF16),
    ]
    return [
        vm(2, 32 * r, 128, dtype=BF16),
        vm(2, 16 * r, 128, dtype=BF16),
        vm(2, 16 * r, 128, dtype=BF16),
        *steps,
        vm(32 * r, 128, dtype=BF16),
    ]


def on_device(*args):
    in_hbm = pl.BlockSpec(memory_space=pltpu.HBM)
    scratch = [
        pltpu.SemaphoreType.DMA((COPIES,)),
        pltpu.SemaphoreType.DMA((COPIES,)),
        pltpu.SemaphoreType.DMA((24,)),
        vm(WIDE, HALF, dtype=BF16),
        vm(WIDE, HALF, dtype=BF16),
        vm(WIDE, HALF, dtype=BF16),
        vm(2, 2, HALF, HALF, dtype=BF16),
        vm(2, WIDE, HID, dtype=BF16),
        vm(2, WIDE, HID, dtype=BF16),
        vm(2, HALF, WIDE, dtype=BF16),
        vm(2, 2, 16, WIDE),
        vm(16, WIDE),
        vm(1, OWN, WIDE, dtype=BF16),
        vm(1, OWN, WIDE, dtype=BF16),
        *[vm(size, dtype=BF16) for size in SMALL],
        vm(2, 4, PAD, WIDE, dtype=BF16),
        vm(4, PAD, WIDE, dtype=BF16),
        vm(2, 4, PAD, WIDE, dtype=BF16),
        vm(4, PAD, WIDE, dtype=BF16),
        vm(4, PAD, 256, dtype=BF16),
        vm(PAD, STACK, dtype=BF16),
        vm(3, WIDE, 256, dtype=BF16),
        vm(2, 256, WIDE, dtype=BF16),
        vm(4, PAD, 256, dtype=BF16),
        vm(4, STACK, 256, dtype=BF16),
        vm(2 * GROUP, 256, dtype=BF16),
        vm(2 * GROUP, 256, dtype=BF16),
        vm(2, 256, GROUP, dtype=BF16),
        vm(2, 256, GROUP, dtype=BF16),
        vm(2, GROUP, 1),
        vm(4, 2 * GROUP, STACK, dtype=BF16),
        vm(4, 1, STACK),
        vm(4, PAD, 256, dtype=BF16),
        vm(3, PAD, 256, dtype=BF16),
        vm(STACK, 256, dtype=BF16),
        vm(1, STACK),
        vm(2 * GROUP, STACK, dtype=BF16),
        vm(2 * GROUP, 256),
        vm(2 * GROUP, 256),
        vm(4, PAD, 256, dtype=BF16),
        vm(3, PAD, 256, dtype=BF16),
        vm(4, PAD, WIDE, dtype=BF16),
        vm(4, PAD, WIDE, dtype=BF16),
        vm(4, PAD, WIDE),
        vm(4, PAD, WIDE, dtype=BF16),
        vm(3, PAD, WIDE, dtype=BF16),
        vm(PAD, WIDE),
        vm(PAD, 1),
        vm(PAD, WIDE, dtype=BF16),
        vm(PAD, WIDE),
        vm(PAD, 256),
        vm(2, PAD, HALF, dtype=BF16),
        vm(PAD, WIDE),
        vm(PAD, WIDE),
        vm(PAD, 1),
        vm(PAD, WIDE, dtype=BF16),
        vm(2, PAD, HID, dtype=BF16),
        vm(2, PAD, HID, dtype=BF16),
        vm(2, PAD, WIDE),
        vm(2, PAD, WIDE, dtype=BF16),
        vm(PAD, WIDE),
        vm(PAD, WIDE),
        *reduction_scratch(UNITS_1, False),
        *reduction_scratch(UNITS_2, True),
        *reduction_scratch(UNITS_3, True),
        vm(2, 2, 16, 128, dtype=BF16),
        vm(OWN, WIDE, dtype=BF16),
        vm(OWN, WIDE),
    ]
    args = list(args)
    args[16] = args[16].T
    specs = [in_hbm] * len(args)
    specs[1] = pl.BlockSpec(memory_space=pltpu.SMEM)
    parts = pl.pallas_call(
        layer_kernel,
        out_shape=[
            jax.ShapeDtypeStruct((OWN, WIDE), BF16),
            jax.ShapeDtypeStruct((OWN, WIDE), F32),
            jax.ShapeDtypeStruct((32 * UNITS_1, 128), BF16),
            jax.ShapeDtypeStruct((32 * UNITS_2, 128), BF16),
            jax.ShapeDtypeStruct((32 * UNITS_3, 128), BF16),
        ],
        in_specs=specs,
        out_specs=[in_hbm] * 5,
        scratch_shapes=scratch,
        compiler_params=pltpu.CompilerParams(
            collective_id=0, has_side_effects=True, vmem_limit_bytes=VMEM_BYTES
        ),
        name="layer",
    )(*args)
    quarter = [
        ((1, OWN, WIDE), BF16), ((1, OWN, WIDE), F32), ((HALF,), F32), ((HALF,), F32), ((HALF, HALF), F32),
        ((96,), F32), ((HALF, HALF), F32), ((HALF, HALF), F32), ((96,), F32), ((HALF, HALF), F32), ((HALF,), F32),
        ((HALF,), F32), ((HALF,), F32), ((HALF, HID), F32), ((WIDE,), F32), ((HALF, HID), F32), ((HALF,), F32),
    ]
    results = list(
        pl.pallas_call(
            finish_kernel,
            out_shape=[jax.ShapeDtypeStruct(shape, dtype) for shape, dtype in quarter],
            in_specs=[in_hbm] * 5,
            out_specs=[in_hbm] * len(quarter),
            scratch_shapes=[
                vm(32 * UNITS_1, 128, dtype=BF16),
                vm(32 * UNITS_2, 128, dtype=BF16),
                vm(32 * UNITS_3, 128, dtype=BF16),
                vm(1, OWN, WIDE),
                vm(1, OWN, WIDE, dtype=BF16),
                *[vm(*shape, dtype=dtype) for shape, dtype in quarter[2:]],
                pltpu.SemaphoreType.DMA((5,)),
                pltpu.SemaphoreType.DMA((17,)),
            ],
            compiler_params=pltpu.CompilerParams(vmem_limit_bytes=VMEM_BYTES),
            name="finish",
        )(*parts)
    )
    results[15] = results[15].T
    return tuple(results)


def solution(mesh):
    wide, split, mixed = P("dp"), P("dp", "tensor"), P(("tensor", "dp"))
    tokens, crossed = P("dp", "ctx", None), P("tensor", "dp")
    return jax.shard_map(
        on_device,
        mesh=mesh,
        in_specs=(
            tokens, P("dp"), tokens, wide, wide, split, mixed, split, split, mixed, crossed, wide,
            wide, wide, split, mixed, crossed, wide,
        ),
        out_specs=(
            tokens, tokens, wide, wide, split, mixed, split, split, mixed, crossed, wide,
            wide, wide, split, mixed, crossed, wide,
        ),
        check_vma=False,
    )
```
